768 devices in a mesh: grp: 12 (over z), own: 64 (over y, x, core).
Axes of the slice: x: 4, y: 8, z: 12, core: 2. Of those that a mesh axis runs over, the one named last changes fastest.
Arguments:
- upstream: bfloat16 [3072, 64, 4, 512], P(('grp', 'own')), may hold values from -6 to 6
- pooled: bfloat16 [3072, 64, 960], P(('grp', 'own')), may hold values from -6 to 6
- projection: bfloat16 [960, 512], replicated, may hold values from -0.5 to 0.5
- embedding: float32 [196608, 960], P(('grp', 'own')), may hold values from -4 to 4
- row_state: float32 [4, 196608], P(None, ('grp', 'own')), may hold values from 0.01 to 1
- lookups: int32 [768, 4, 256, 16], P(('grp', 'own')), may hold values from 0 to 255
- bag_sizes: int32 [768, 4, 256], P(('grp', 'own')), may hold values from 1 to 16, as said below
Outputs:
- updated_rows: float32 [196608, 960], P(('grp', 'own'))
- updated_state: float32 [4, 196608], P(None, ('grp', 'own'))
- proj_grad: float32 [960, 512], replicated
The draws below stay inside these ranges and needn't reach their ends.
Inputs may be any that keep to these rules, and one draw needn't show every extreme that they name: `bag_sizes`: positions at or past a bag's size are not looked up.
All inputs are finite; a program needn't handle non-finite values.
Results may differ from the reference program's by a relative error of at most 0.00051.
Values may be sent and summed in bfloat16 or wider, within the bound.
A program may use at most 32 MiB of HBM per device.

```python
import math
import jax
import jax.numpy as jnp
import numpy as np
from jax import lax

DIM_A = 64
DIM_B = 128
DIM_C = 256
DIM_D = 512
PROJ = 512
BAG = 16
ROWS = 256
DSUM = 960
GB = 256
SAMPLES = 3072
OWNERS = 768
PEERS = 64
N_GRP = 12
N_OWN = 64


def draw_bag_sizes(key, part):
    key = jax.random.fold_in(key, 7)
    key_one, key_two = jax.random.split(key)
    longest = jax.random.randint(key_one, (OWNERS, 4, 1), max(1, BAG // 4), BAG + 1)
    leader = (lax.broadcasted_iota(jnp.int32, (OWNERS, 4, 1), 0) == 0) & (lax.broadcasted_iota(jnp.int32, (OWNERS, 4, 1), 1) == 0)
    longest = jnp.where(leader, BAG, longest)
    lengths = jax.random.randint(key_two, (OWNERS, 4, GB), 1, longest + 1)
    column = lax.broadcasted_iota(jnp.int32, (OWNERS, 4, GB), 2)
    return jnp.where(column == 0, jnp.broadcast_to(longest, (OWNERS, 4, GB)), lengths).astype(jnp.int32)


def with_ends(entries, key, smallest, high):
    dims = entries.shape
    index_at = [jax.random.randint(jax.random.fold_in(key, axis), (), 0, dims[axis]) for axis in range(len(dims))]
    entries = entries.at[tuple(index_at)].set(smallest)
    longest = dims.index(max(dims))
    index_at[longest] = (index_at[longest] + 1) % dims[longest]
    return entries.at[tuple(index_at)].set(high)


def block_levels(rng, dims, shards, smallest, top_value):
    def one(position, shards_of):
        heights = jax.random.uniform(jax.random.fold_in(jax.random.fold_in(rng, 6), position), (shards_of,), jnp.float32, smallest / len(shards), top_value / len(shards))
        return jnp.repeat(jnp.exp(heights), dims[position] // shards_of).reshape((-1,) + (1,) * (len(dims) - position - 1))

    factor_of = one(*shards[0])
    for cut in shards[1:]:
        factor_of = factor_of * one(*cut)
    return factor_of


def rank_bounds(number_of, skew):
    portions = [(1 << 20) // math.isqrt(rank ** skew) + 1 for rank in range(1, number_of + 1)]
    spread = 1 + sum(portions) // (1 << 30)
    return np.cumsum(np.array([max(1, weight // spread) for weight in portions]))


def ranked(own_key, dims, count, lean):
    grid = rank_bounds(count, lean)
    pick = jax.random.randint(jax.random.fold_in(own_key, 1), dims, 0, int(grid[count - 1]))
    rank = jnp.searchsorted(jnp.asarray(grid, jnp.int32), pick, side="right")
    return jax.random.permutation(jax.random.fold_in(own_key, 2), count)[rank].astype(jnp.int32)


def scatter_about(stream_key, dims, width, most, shards=(), kind=jnp.bfloat16):
    gain = block_levels(stream_key, dims, shards, -0.22, 0.18) if shards else 1.0
    entries = jax.random.normal(stream_key, dims, jnp.float32) * width * gain
    return jnp.minimum(jnp.maximum(entries, -most), most).astype(kind)


def setup_inputs(seed: int = 0) -> dict:
    seeds = jax.random.split(jax.random.key(seed), 8)
    return {
        "upstream": scatter_about(seeds[0], (SAMPLES, PEERS, 4, PROJ), 1.0, 6.0, ((0, 768),)),
        "pooled": scatter_about(seeds[1], (SAMPLES, PEERS, DSUM), 1.0, 6.0, ((0, 768),)),
        "projection": scatter_about(seeds[2], (DSUM, PROJ), DIM_B ** -0.5, 0.5),
        "embedding": scatter_about(seeds[3], (OWNERS * ROWS, DSUM), 0.5, 4.0, ((0, 768),), jnp.float32),
        "row_state": jnp.clip(jnp.exp(math.log(1.0) - 4.6051702 * jax.random.uniform(seeds[4], (4, OWNERS * ROWS), jnp.float32) ** block_levels(seeds[4], (4, OWNERS * ROWS), ((1, 768),), -0.2, 0.2)), 0.01, 1.0),
        "lookups": with_ends(ranked(seeds[5], (OWNERS, 4, GB, BAG), ROWS, 2), jax.random.fold_in(seeds[5], 3), 0, ROWS - 1).astype(jnp.int32),
        "bag_sizes": draw_bag_sizes(jax.random.fold_in(seeds[7], 71), 0),
    }


LEARN = 0.05

def column_blocks():
    blocks = []
    offset = 0
    for breadth in (DIM_A, DIM_B, DIM_C, DIM_D):
        blocks.append((offset, breadth))
        offset += breadth
    return blocks

def narrowed(grads, projection):
    pieces = []
    for member, (offset, breadth) in enumerate(column_blocks()):
        weight_block = projection[offset:offset + breadth].astype(jnp.float32)
        pieces.append(jnp.einsum('...e,ke->...k', grads[..., member, :].astype(jnp.float32), weight_block))
    return jnp.concatenate(pieces, axis=-1).astype(jnp.bfloat16)

def reference(upstream, pooled, projection, embedding, row_state, lookups, bag_sizes):

    def group_term(total, group):
        start = (group * GB).astype(jnp.int32)
        pooled_block = lax.dynamic_slice_in_dim(pooled, start, GB, 0).astype(jnp.float32)
        upper_block = lax.dynamic_slice_in_dim(upstream, start, GB, 0).astype(jnp.float32)
        pieces = []
        for member, (offset, breadth) in enumerate(column_blocks()):
            pieces.append(jnp.einsum('sok,soe->ke', pooled_block[:, :, offset:offset + breadth], upper_block[:, :, member, :]))
        return (total + jnp.concatenate(pieces, axis=0), None)
    summed, unused = lax.scan(group_term, jnp.zeros((DSUM, PROJ), jnp.float32), jnp.arange(N_GRP, dtype=jnp.int32))
    proj_grad = summed * (1.0 / math.sqrt(SAMPLES * PEERS))

    def owner_update(items):
        number, rows_here, state_here, picks, counts = items
        group = number // N_OWN
        owner = number % N_OWN
        block = lax.dynamic_slice_in_dim(upstream, (group * GB).astype(jnp.int32), GB, 0)
        mine = lax.dynamic_index_in_dim(block, owner, 1, keepdims=False)
        bag_grad = narrowed(mine, projection)
        new_rows = []
        new_state = []
        positions = jnp.arange(BAG, dtype=jnp.int32)
        for member, (offset, breadth) in enumerate(column_blocks()):
            valid = positions[None, :] < counts[member][:, None]
            values = jnp.where(valid[:, :, None], bag_grad[:, None, offset:offset + breadth].astype(jnp.float32), 0.0)
            grad = jax.ops.segment_sum(values.reshape(GB * BAG, breadth), picks[member].reshape(GB * BAG), num_segments=ROWS)
            state = state_here[member] + lax.optimization_barrier(jnp.mean(grad * grad, axis=1))
            new_state.append(state)
            new_rows.append(rows_here[:, offset:offset + breadth] - LEARN * grad / jnp.sqrt(state)[:, None])
        return (jnp.concatenate(new_rows, axis=1), jnp.stack(new_state, axis=0))
    rows_all = embedding.reshape(OWNERS, ROWS, DSUM)
    state_all = jnp.transpose(row_state.reshape(4, OWNERS, ROWS), (1, 0, 2))
    new_rows, new_state = lax.map(owner_update, (jnp.arange(OWNERS, dtype=jnp.int32), rows_all, state_all, lookups, bag_sizes))
    updated_rows = new_rows.reshape(OWNERS * ROWS, DSUM)
    updated_state = jnp.transpose(new_state, (1, 0, 2)).reshape(4, OWNERS * ROWS)
    return (updated_rows, updated_state, proj_grad)
```

```python
import functools
import math

import jax
import jax.numpy as jnp
from jax import lax
from jax.experimental import pallas as pl
from jax.experimental.pallas import tpu as pltpu
from jax.sharding import PartitionSpec as P

BAG = 16
GB = 256
LEARN = 0.05
NX, NY, NZ = 4, 8, 12
N_OWN = 64
MESH = pl.DeviceIdType.MESH
F32 = jnp.float32
BF16 = jnp.bfloat16
CLASSES = ((0, 64), (64, 128), (192, 256), (448, 512))
BLOCKS = ((0, 1), (1, 1), (2, 2), (4, 4))


def kernel(
    ua, ub, uc, ud, pooled, proj, emb, state, looks, sizes,
    rows_out, state_out, pg_out,
    ua_v, ub_v, uc_v, ud_v, pooled_v, proj_v, emb_v, state_v, looks_v, sizes_v,
    acc, sib, xs, xr, ys, yr, z1, z2, pg,
    stage, abuf, arecv, tal, rows_v, state_new,
    in_sem, sib_s, sib_r, x_s, x_r, y_s, y_r, z1_s, z1_r, z2_s, z2_r,
    a_s, a_r, gy_s, gy_r, gx_s, gx_r, gs_s, gs_r, out_sem,
):
    g = lax.axis_index("grp")
    p = lax.axis_index("own")
    core = lax.rem(p, 2)
    xi = lax.rem(p // 2, NX)
    yi = p // (2 * NX)
    zq = g // 4
    zi = lax.rem(g, 4)
    other = 1 - core

    def at(y, x, c):
        return (g, (y * NX + x) * 2 + c)

    def remote(src, dst, send, recv, dev):
        return pltpu.make_async_remote_copy(
            src_ref=src, dst_ref=dst, send_sem=send, recv_sem=recv,
            device_id=dev, device_id_type=MESH,
        )

    ins = (
        (ua, ua_v), (ub, ub_v), (uc, uc_v), (ud, ud_v), (pooled, pooled_v),
        (proj, proj_v), (looks, looks_v), (sizes, sizes_v), (emb, emb_v), (state, state_v),
    )
    loads = [pltpu.make_async_copy(a, b, in_sem.at[i]) for i, (a, b) in enumerate(ins)]
    for load in loads:
        load.start()

    barrier = pltpu.get_barrier_semaphore()

    @pl.loop(1, N_OWN)
    def _(i):
        pl.semaphore_signal(barrier, inc=1, device_id=(g, lax.rem(p + i, N_OWN)), device_id_type=MESH)

    def z_near(i):
        return (zq * 4 + lax.rem(zi + i, 4), p)

    def z_far(i):
        return (lax.rem(g + 4 * i, NZ), p)

    for i in (1, 2, 3):
        pl.semaphore_signal(barrier, inc=1, device_id=z_near(i), device_id_type=MESH)
    for i in (1, 2):
        pl.semaphore_signal(barrier, inc=1, device_id=z_far(i), device_id_type=MESH)

    for load in loads[:5]:
        load.wait()

    def term(lo, hi, u):
        return lax.dot_general(
            pooled_v[:, lo:hi], u[...], (((0,), (0,)), ((), ())), preferred_element_type=F32
        )

    acc[0] = term(384, 960, ud_v)[64:576]
    acc[1, 0:128] = term(0, 128, ua_v)
    acc[1, 128:256] = term(0, 256, ub_v)[64:192]
    acc[1, 256:512] = term(128, 512, uc_v)[64:320]

    pl.semaphore_wait(barrier, N_OWN - 1 + 5)

    sib_dev = at(yi, xi, other)
    sib_copies = []
    for i in (2, 1, 3, 0):
        t = lax.rem(xi + i, NX)
        rows = pl.ds(pl.multiple_of(t * 128, 128), 128)
        copy = remote(acc.at[other, rows], sib.at[rows], sib_s.at[i], sib_r.at[i], sib_dev)
        copy.start()
        sib_copies.append((i, rows, t, copy))

    x_copies = []
    for i, rows, t, copy in sib_copies:
        copy.wait_recv()
        if i == 0:
            break
        xs[i - 1] = acc[core, rows] + sib[rows]
        out = remote(xs.at[i - 1], xr.at[i - 1], x_s.at[i - 1], x_r.at[i - 1], at(yi, t, core))
        out.start()
        x_copies.append(out)
    own_rows = sib_copies[3][1]

    loads[5].wait()
    for u, (offset, width), (block, number) in zip((ua_v, ub_v, uc_v, ud_v), CLASSES, BLOCKS):
        bag = lax.dot_general(
            u[...], proj_v[offset : offset + number * 128], (((1,), (1,)), ((), ())),
            preferred_element_type=F32,
        )
        for k in range(number):
            for s in range(4):
                stage[pl.ds(s * 8 + block + k, N_OWN, stride=32), :] = bag[
                    s * 64 : s * 64 + 64, k * 128 : k * 128 + 128
                ]
    abuf[...] = stage[...].reshape(N_OWN, 32, 128).astype(BF16)

    loads[6].wait()
    loads[7].wait()
    spread = lax.broadcasted_iota(jnp.int32, (GB, GB), 0)
    order = (spread & 63) * 4 + (spread >> 6)
    picked = jnp.where(order == lax.broadcasted_iota(jnp.int32, (GB, GB), 1), 1.0, 0.0).astype(BF16)
    for member in range(4):
        valid = lax.broadcasted_iota(jnp.int32, (BAG, GB), 0) < sizes_v[member : member + 1, :]
        wanted = jnp.where(valid, looks_v[member], -1)
        parts = []
        for r in range(0, GB, 64):
            ids = lax.broadcasted_iota(jnp.int32, (64, GB), 0) + r
            count = jnp.zeros((64, GB), F32)
            for l in range(BAG):
                count += jnp.where(wanted[l : l + 1, :] == ids, 1.0, 0.0)
            parts.append(count.astype(BF16))
        counts = jnp.concatenate(parts, axis=0)
        tal[member] = lax.dot_general(
            picked, counts, (((1,), (1,)), ((), ())), preferred_element_type=F32
        ).astype(BF16)

    total = acc[core, own_rows] + sib[own_rows]
    for i, copy in zip((2, 1, 3), x_copies):
        copy.wait_recv()
        total += xr[i - 1]
    for y in range(NY):
        ys[y] = total[y * 16 : y * 16 + 16]

    y_copies = []
    for i in (4, 3, 5, 2, 6, 1, 7):
        t = lax.rem(yi + i, NY)
        copy = remote(ys.at[t], yr.at[i - 1], y_s.at[i - 1], y_r.at[i - 1], at(t, xi, core))
        copy.start()
        y_copies.append((i, copy))

    def to_owner(i):
        t = lax.rem(p + i, N_OWN)
        return remote(abuf.at[t], arecv.at[p], a_s, a_r, (g, t))

    @pl.loop(1, N_OWN)
    def _(i):
        to_owner(i).start()

    arecv[p] = abuf[p]

    part = ys[yi]
    for i, copy in y_copies:
        copy.wait_recv()
        part += yr[i - 1]

    z1[zi] = part
    z1_copies = []
    for i in (1, 2, 3):
        copy = remote(z1.at[zi], z1.at[zi], z1_s.at[i - 1], z1_r.at[i - 1], z_near(i))
        copy.start()
        z1_copies.append(copy)
    for copy in z1_copies:
        copy.wait_recv()
    z2[zq] = (z1[0] + z1[1]) + (z1[2] + z1[3])
    z2_copies = []
    for i in (1, 2):
        copy = remote(z2.at[zq], z2.at[zq], z2_s.at[i - 1], z2_r.at[i - 1], z_far(i))
        copy.start()
        z2_copies.append(copy)
    for copy in z2_copies:
        copy.wait_recv()
    first = core * 32
    mine = first + xi * 8 + yi
    pg[mine] = (z2[0] + z2[1]) + z2[2]

    gy_copies = []
    for i in (4, 3, 5, 2, 6, 1, 7):
        t = lax.rem(yi + i, NY)
        copy = remote(pg.at[mine], pg.at[mine], gy_s.at[i - 1], gy_r.at[i - 1], at(t, xi, core))
        copy.start()
        gy_copies.append(copy)

    pltpu.make_async_copy(arecv.at[pl.ds(0, N_OWN - 1)], arecv.at[pl.ds(0, N_OWN - 1)], a_r).wait()
    loads[8].wait()
    loads[9].wait()
    stage[...] = arecv[...].astype(F32).reshape(N_OWN * 32, 128)
    for member, ((offset, width), (block, number)) in enumerate(zip(CLASSES, BLOCKS)):
        columns = []
        for k in range(number):
            columns.append(
                jnp.concatenate(
                    [stage[pl.ds(s * 8 + block + k, N_OWN, stride=32), :] for s in range(4)], axis=0
                ).astype(BF16)
            )
        bags = columns[0] if number == 1 else jnp.concatenate(columns, axis=1)
        grad = lax.dot_general(
            bags, tal[member], (((0,), (0,)), ((), ())), preferred_element_type=F32
        )[:width]
        new = state_v[member : member + 1, :] + jnp.sum(grad * grad, axis=0, keepdims=True) * (1.0 / width)
        state_new[member : member + 1, :] = new
        rows_v[offset : offset + width, :] = emb_v[offset : offset + width, :] - grad * (LEARN / jnp.sqrt(new))
    outs = [
        pltpu.make_async_copy(rows_v, rows_out, out_sem.at[0]),
        pltpu.make_async_copy(state_new, state_out, out_sem.at[1]),
    ]
    for out in outs:
        out.start()

    for copy in gy_copies:
        copy.wait_recv()

    def chunk(t):
        return pg.at[pl.ds(first + t * 8, 8)]

    gx_copies = []
    for i in (2, 1, 3):
        t = lax.rem(xi + i, NX)
        copy = remote(chunk(xi), chunk(xi), gx_s.at[i - 1], gx_r.at[i - 1], at(yi, t, core))
        copy.start()
        gx_copies.append((i, copy))
    gs_copies = [remote(chunk(xi), chunk(xi), gs_s.at[0], gs_r.at[0], sib_dev)]
    gs_copies[0].start()
    for i, copy in sorted(gx_copies, key=lambda pair: pair[0] % 2 == 0):
        copy.wait_recv()
        t = lax.rem(xi - i + NX, NX)
        hand = remote(chunk(t), chunk(t), gs_s.at[i], gs_r.at[i], sib_dev)
        hand.start()
        gs_copies.append(hand)
    for hand in gs_copies:
        hand.wait_recv()
    for i, (src, dst, number) in enumerate(((0, 28, 32), (32, 0, 4), (40, 4, 24))):
        out = pltpu.make_async_copy(
            pg.at[pl.ds(src, number)], pg_out.at[pl.ds(dst, number)], out_sem.at[2 + i]
        )
        out.start()
        outs.append(out)

    for group in ([c[3] for c in sib_copies], x_copies, [c for _, c in y_copies], z1_copies, z2_copies,
                  gy_copies, [c for _, c in gx_copies], gs_copies):
        for copy in group:
            copy.wait_send()

    @pl.loop(1, N_OWN)
    def _(i):
        to_owner(i).wait_send()

    for out in outs:
        out.wait()


def on_device(upstream, pooled, projection, embedding, row_state, lookups, bag_sizes):
    ups = [upstream[:, :, c, :].reshape(GB, 512) for c in range(4)]
    operands = (
        *ups, pooled.reshape(GB, 960), projection, embedding.T, row_state,
        jnp.transpose(lookups[0], (0, 2, 1)), bag_sizes[0],
    )
    dma = pltpu.SemaphoreType.DMA
    any_space = pl.BlockSpec(memory_space=pl.ANY)
    scratch = [pltpu.VMEM(a.shape, a.dtype) for a in operands] + [
        pltpu.VMEM((2, 512, 512), F32),
        pltpu.VMEM((512, 512), F32),
        pltpu.VMEM((3, 128, 512), F32),
        pltpu.VMEM((3, 128, 512), F32),
        pltpu.VMEM((8, 16, 512), F32),
        pltpu.VMEM((7, 16, 512), F32),
        pltpu.VMEM((4, 16, 512), F32),
        pltpu.VMEM((3, 16, 512), F32),
        pltpu.VMEM((64, 16, 512), F32),
        pltpu.VMEM((N_OWN * 32, 128), F32),
        pltpu.VMEM((N_OWN, 32, 128), BF16),
        pltpu.VMEM((N_OWN, 32, 128), BF16),
        pltpu.VMEM((4, GB, GB), BF16),
        pltpu.VMEM((960, GB), F32),
        pltpu.VMEM((4, GB), F32),
        dma((10,)),
        dma((4,)), dma((4,)), dma((3,)), dma((3,)), dma((7,)), dma((7,)),
        dma((3,)), dma((3,)), dma((2,)), dma((2,)),
        dma, dma, dma((7,)), dma((7,)), dma((3,)), dma((3,)), dma((4,)), dma((4,)), dma((5,)),
    ]
    rows_t, new_state, pg = pl.pallas_call(
        kernel,
        out_shape=(
            jax.ShapeDtypeStruct((960, GB), F32),
            jax.ShapeDtypeStruct((4, GB), F32),
            jax.ShapeDtypeStruct((60, 16, 512), F32),
        ),
        in_specs=[any_space] * len(operands),
        out_specs=(any_space,) * 3,
        scratch_shapes=scratch,
        compiler_params=pltpu.CompilerParams(
            collective_id=0, has_side_effects=True, vmem_limit_bytes=40 * 2**20
        ),
        name="fused",
    )(*operands)
    total_bags = upstream.shape[0] * lax.axis_size("grp") * lax.axis_size("own") * upstream.shape[1]
    return rows_t.T, new_state, pg.reshape(960, 512) * (1.0 / math.sqrt(total_bags))


def solution(mesh):
    return jax.shard_map(
        on_device,
        mesh=mesh,
        in_specs=(
            P(("grp", "own"), None, None, None),
            P(("grp", "own"), None, None),
            P(),
            P(("grp", "own"), None),
            P(None, ("grp", "own")),
            P(("grp", "own"), None, None, None),
            P(("grp", "own"), None, None),
        ),
        out_specs=(P(("grp", "own"), None), P(None, ("grp", "own")), P()),
        check_vma=False,
    )
```

```python
import functools
import math

import jax
import jax.numpy as jnp
from jax import lax
from jax.experimental import pallas as pl
from jax.experimental.pallas import tpu as pltpu
from jax.sharding import PartitionSpec as P

BAG = 16
GB = 256
LEARN = 0.05
NX, NY, NZ = 4, 8, 12
N_OWN = 64
MESH = pl.DeviceIdType.MESH
F32 = jnp.float32
BF16 = jnp.bfloat16
CLASSES = ((0, 64), (64, 128), (192, 256), (448, 512))
BLOCKS = ((0, 1), (1, 1), (2, 2), (4, 4))


def kernel(
    scale,
    ups, pooled, proj, emb, state, looks, sizes,
    rows_out, state_out, pg_out,
    ups_v, pooled_v, proj_v, emb_v, state_v, looks_v, sizes_v,
    acc, sib, xs, xr, ys, yr, z1, z2, pg,
    wide, uc_v, stage, abuf, arecv, tal, rows_v, state_new,
    in_sem, sib_s, sib_r, x_s, x_r, y_s, y_r, z1_s, z1_r, z2_s, z2_r,
    a_s, a_r, gy_s, gy_r, gx_s, gx_r, gs_s, gs_r, out_sem,
):
    g = lax.axis_index("grp")
    p = lax.axis_index("own")
    core = lax.rem(p, 2)
    xi = lax.rem(p // 2, NX)
    yi = p // (2 * NX)
    zq = g // 4
    zi = lax.rem(g, 4)
    other = 1 - core

    def at(y, x, c):
        return (g, (y * NX + x) * 2 + c)

    def remote(src, dst, send, recv, dev):
        return pltpu.make_async_remote_copy(
            src_ref=src, dst_ref=dst, send_sem=send, recv_sem=recv,
            device_id=dev, device_id_type=MESH,
        )

    ins = (
        (ups, ups_v), (pooled, pooled_v), (proj, proj_v), (looks, looks_v), (sizes, sizes_v), (emb, emb_v), (state, state_v),
    )
    loads = [pltpu.make_async_copy(a, b, in_sem.at[i]) for i, (a, b) in enumerate(ins)]
    for load in loads:
        load.start()

    barrier = pltpu.get_barrier_semaphore()

    @pl.loop(1, N_OWN)
    def _(i):
        pl.semaphore_signal(barrier, inc=1, device_id=(g, lax.rem(p + i, N_OWN)), device_id_type=MESH)

    def z_near(i):
        return (zq * 4 + lax.rem(zi + i, 4), p)

    def z_far(i):
        return (lax.rem(g + 4 * i, NZ), p)

    for i in (1, 2, 3):
        pl.semaphore_signal(barrier, inc=1, device_id=z_near(i), device_id_type=MESH)
    for i in (1, 2):
        pl.semaphore_signal(barrier, inc=1, device_id=z_far(i), device_id_type=MESH)

    for load in loads[:1]:
        load.wait()

    @pl.loop(0, 8)
    def _(b):
        some = ups_v[pl.ds(b * 32, 32)].astype(F32)
        for t in range(4):
            wide[t, pl.ds(pl.multiple_of(b * 128, 128), 128), :] = some[:, :, t * 128 : t * 128 + 128].reshape(128, 128)

    for c in range(4):
        for t in range(4):
            uc_v[c, :, t * 128 : t * 128 + 128] = wide[t, pl.ds(c, GB, stride=4), :].astype(BF16)

    loads[1].wait()

    def term(lo, hi, c):
        return lax.dot_general(
            pooled_v[:, lo:hi], uc_v[c], (((0,), (0,)), ((), ())), preferred_element_type=F32
        )

    acc[0] = term(384, 960, 3)[64:576]
    acc[1, 0:128] = term(0, 128, 0)
    acc[1, 128:256] = term(0, 256, 1)[64:192]
    acc[1, 256:512] = term(128, 512, 2)[64:320]

    pl.semaphore_wait(barrier, N_OWN - 1 + 5)

    sib_dev = at(yi, xi, other)
    sib_copies = []
    for i in (2, 1, 3, 0):
        t = lax.rem(xi + i, NX)
        rows = pl.ds(pl.multiple_of(t * 128, 128), 128)
        copy = remote(acc.at[other, rows], sib.at[rows], sib_s.at[i], sib_r.at[i], sib_dev)
        copy.start()
        sib_copies.append((i, rows, t, copy))

    x_copies = []
    for i, rows, t, copy in sib_copies:
        copy.wait_recv()
        if i == 0:
            break
        xs[i - 1] = acc[core, rows] + sib[rows]
        out = remote(xs.at[i - 1], xr.at[i - 1], x_s.at[i - 1], x_r.at[i - 1], at(yi, t, core))
        out.start()
        x_copies.append(out)
    own_rows = sib_copies[3][1]

    loads[2].wait()
    for c, ((offset, width), (block, number)) in enumerate(zip(CLASSES, BLOCKS)):
        bag = lax.dot_general(
            uc_v[c], proj_v[offset : offset + number * 128], (((1,), (1,)), ((), ())),
            preferred_element_type=F32,
        )
        for k in range(number):
            for s in range(4):
                stage[pl.ds(s * 8 + block + k, N_OWN, stride=32), :] = bag[
                    s * 64 : s * 64 + 64, k * 128 : k * 128 + 128
                ]
    abuf[...] = stage[...].reshape(N_OWN, 32, 128).astype(BF16)

    loads[3].wait()
    loads[4].wait()
    spread = lax.broadcasted_iota(jnp.int32, (GB, GB), 0)
    order = (spread & 63) * 4 + (spread >> 6)
    picked = jnp.where(order == lax.broadcasted_iota(jnp.int32, (GB, GB), 1), 1.0, 0.0).astype(BF16)
    for member in range(4):
        valid = lax.broadcasted_iota(jnp.int32, (BAG, GB), 0) < sizes_v[member : member + 1, :]
        wanted = jnp.where(valid, looks_v[member], -1)
        parts = []
        for r in range(0, GB, 64):
            ids = lax.broadcasted_iota(jnp.int32, (64, GB), 0) + r
            count = jnp.zeros((64, GB), F32)
            for l in range(BAG):
                count += jnp.where(wanted[l : l + 1, :] == ids, 1.0, 0.0)
            parts.append(count.astype(BF16))
        counts = jnp.concatenate(parts, axis=0)
        tal[member] = lax.dot_general(
            picked, counts, (((1,), (1,)), ((), ())), preferred_element_type=F32
        ).astype(BF16)

    total = acc[core, own_rows] + sib[own_rows]
    for i, copy in zip((2, 1, 3), x_copies):
        copy.wait_recv()
        total += xr[i - 1]
    for y in range(NY):
        ys[y] = total[y * 16 : y * 16 + 16]

    y_copies = []
    for i in (4, 3, 5, 2, 6, 1, 7):
        t = lax.rem(yi + i, NY)
        copy = remote(ys.at[t], yr.at[i - 1], y_s.at[i - 1], y_r.at[i - 1], at(t, xi, core))
        copy.start()
        y_copies.append((i, copy))

    def to_owner(i):
        t = lax.rem(p + i, N_OWN)
        return remote(abuf.at[t], arecv.at[p], a_s, a_r, (g, t))

    @pl.loop(1, N_OWN)
    def _(i):
        to_owner(i).start()

    arecv[p] = abuf[p]

    part = ys[yi]
    for i, copy in y_copies:
        copy.wait_recv()
        part += yr[i - 1]

    z1[zi] = part
    z1_copies = []
    for i in (1, 2, 3):
        copy = remote(z1.at[zi], z1.at[zi], z1_s.at[i - 1], z1_r.at[i - 1], z_near(i))
        copy.start()
        z1_copies.append(copy)
    for copy in z1_copies:
        copy.wait_recv()
    z2[zq] = (z1[0] + z1[1]) + (z1[2] + z1[3])
    z2_copies = []
    for i in (1, 2):
        copy = remote(z2.at[zq], z2.at[zq], z2_s.at[i - 1], z2_r.at[i - 1], z_far(i))
        copy.start()
        z2_copies.append(copy)
    for copy in z2_copies:
        copy.wait_recv()
    first = core * 32
    mine = first + xi * 8 + yi
    pg[mine] = ((z2[0] + z2[1]) + z2[2]) * scale

    gy_copies = []
    for i in (4, 3, 5, 2, 6, 1, 7):
        t = lax.rem(yi + i, NY)
        copy = remote(pg.at[mine], pg.at[mine], gy_s.at[i - 1], gy_r.at[i - 1], at(t, xi, core))
        copy.start()
        gy_copies.append(copy)

    pltpu.make_async_copy(arecv.at[pl.ds(0, N_OWN - 1)], arecv.at[pl.ds(0, N_OWN - 1)], a_r).wait()
    loads[5].wait()
    loads[6].wait()
    stage[...] = arecv[...].astype(F32).reshape(N_OWN * 32, 128)
    for member, ((offset, width), (block, number)) in enumerate(zip(CLASSES, BLOCKS)):
        columns = []
        for k in range(number):
            columns.append(
                jnp.concatenate(
                    [stage[pl.ds(s * 8 + block + k, N_OWN, stride=32), :] for s in range(4)], axis=0
                ).astype(BF16)
            )
        bags = columns[0] if number == 1 else jnp.concatenate(columns, axis=1)
        grad = lax.dot_general(
            bags, tal[member], (((0,), (0,)), ((), ())), preferred_element_type=F32
        )[:width]
        new = state_v[member : member + 1, :] + jnp.sum(grad * grad, axis=0, keepdims=True) * (1.0 / width)
        state_new[member : member + 1, :] = new
        rows_v[offset : offset + width, :] = emb_v[offset : offset + width, :] - grad * (LEARN / jnp.sqrt(new))
    outs = [
        pltpu.make_async_copy(rows_v, rows_out, out_sem.at[0]),
        pltpu.make_async_copy(state_new, state_out, out_sem.at[1]),
    ]
    for out in outs:
        out.start()

    for copy in gy_copies:
        copy.wait_recv()

    def chunk(t):
        return pg.at[pl.ds(first + t * 8, 8)]

    gx_copies = []
    for i in (2, 1, 3):
        t = lax.rem(xi + i, NX)
        copy = remote(chunk(xi), chunk(xi), gx_s.at[i - 1], gx_r.at[i - 1], at(yi, t, core))
        copy.start()
        gx_copies.append((i, copy))
    gs_copies = [remote(chunk(xi), chunk(xi), gs_s.at[0], gs_r.at[0], sib_dev)]
    gs_copies[0].start()
    for i, copy in sorted(gx_copies, key=lambda pair: pair[0] % 2 == 0):
        copy.wait_recv()
        t = lax.rem(xi - i + NX, NX)
        hand = remote(chunk(t), chunk(t), gs_s.at[i], gs_r.at[i], sib_dev)
        hand.start()
        gs_copies.append(hand)
    for hand in gs_copies:
        hand.wait_recv()
    for i, (src, dst, number) in enumerate(((0, 28, 32), (32, 0, 4), (40, 4, 24))):
        out = pltpu.make_async_copy(
            pg.at[pl.ds(src, number)], pg_out.at[pl.ds(dst, number)], out_sem.at[2 + i]
        )
        out.start()
        outs.append(out)

    for group in ([c[3] for c in sib_copies], x_copies, [c for _, c in y_copies], z1_copies, z2_copies,
                  gy_copies, [c for _, c in gx_copies], gs_copies):
        for copy in group:
            copy.wait_send()

    @pl.loop(1, N_OWN)
    def _(i):
        to_owner(i).wait_send()

    for out in outs:
        out.wait()


def flush(rows, state, pg, rows_out, state_out, pg_out, sem):
    pairs = ((pg, pg_out), (rows, rows_out), (state, state_out))
    copies = [pltpu.make_async_copy(a, b, sem.at[i]) for i, (a, b) in enumerate(pairs)]
    for copy in copies:
        copy.start()
    for copy in copies:
        copy.wait()


def on_device(upstream, pooled, projection, embedding, row_state, lookups, bag_sizes):
    total_bags = upstream.shape[0] * lax.axis_size("grp") * lax.axis_size("own") * upstream.shape[1]
    scale = 1.0 / math.sqrt(total_bags)
    operands = (
        upstream.reshape(GB, 4, 512), pooled.reshape(GB, 960), projection, embedding.T, row_state,
        jnp.transpose(lookups[0], (0, 2, 1)), bag_sizes[0],
    )
    dma = pltpu.SemaphoreType.DMA
    any_space = pl.BlockSpec(memory_space=pl.ANY)
    scratch = [pltpu.VMEM(a.shape, a.dtype) for a in operands] + [
        pltpu.VMEM((2, 512, 512), F32),
        pltpu.VMEM((512, 512), F32),
        pltpu.VMEM((3, 128, 512), F32),
        pltpu.VMEM((3, 128, 512), F32),
        pltpu.VMEM((8, 16, 512), F32),
        pltpu.VMEM((7, 16, 512), F32),
        pltpu.VMEM((4, 16, 512), F32),
        pltpu.VMEM((3, 16, 512), F32),
        pltpu.VMEM((64, 16, 512), F32),
        pltpu.VMEM((4, 4 * GB, 128), F32),
        pltpu.VMEM((4, GB, 512), BF16),
        pltpu.VMEM((N_OWN * 32, 128), F32),
        pltpu.VMEM((N_OWN, 32, 128), BF16),
        pltpu.VMEM((N_OWN, 32, 128), BF16),
        pltpu.VMEM((4, GB, GB), BF16),
        pltpu.VMEM((960, GB), F32),
        pltpu.VMEM((4, GB), F32),
        dma((7,)),
        dma((4,)), dma((4,)), dma((3,)), dma((3,)), dma((7,)), dma((7,)),
        dma((3,)), dma((3,)), dma((2,)), dma((2,)),
        dma, dma, dma((7,)), dma((7,)), dma((3,)), dma((3,)), dma((4,)), dma((4,)), dma((5,)),
    ]
    rows_t, new_state, pg = pl.pallas_call(
        functools.partial(kernel, scale),
        out_shape=(
            pltpu.VMEM((960, GB), F32),
            pltpu.VMEM((4, GB), F32),
            pltpu.VMEM((60, 16, 512), F32),
        ),
        in_specs=[pl.BlockSpec(memory_space=pltpu.HBM)] * len(operands),
        out_specs=(any_space,) * 3,
        scratch_shapes=scratch,
        compiler_params=pltpu.CompilerParams(
            collective_id=0, has_side_effects=True, vmem_limit_bytes=54 * 2**20
        ),
        name="fused",
    )(*operands)
    outs = (rows_t, new_state, pg)
    rows_t, new_state, pg = pl.pallas_call(
        flush,
        out_shape=tuple(jax.ShapeDtypeStruct(a.shape, a.dtype) for a in outs),
        in_specs=[any_space] * 3,
        out_specs=(any_space,) * 3,
        scratch_shapes=[dma((3,))],
        name="flush",
    )(*outs)
    return rows_t.T, new_state, pg.reshape(960, 512)


def solution(mesh):
    return jax.shard_map(
        on_device,
        mesh=mesh,
        in_specs=(
            P(("grp", "own"), None, None, None),
            P(("grp", "own"), None, None),
            P(),
            P(("grp", "own"), None),
            P(None, ("grp", "own")),
            P(("grp", "own"), None, None, None),
            P(("grp", "own"), None, None),
        ),
        out_specs=(P(("grp", "own"), None), P(None, ("grp", "own")), P()),
        check_vma=False,
    )
```

```python
import functools
import math

import jax
import jax.numpy as jnp
from jax import lax
from jax.experimental import pallas as pl
from jax.experimental.pallas import tpu as pltpu
from jax.sharding import PartitionSpec as P

BAG = 16
GB = 256
LEARN = 0.05
NX, NY, NZ = 4, 8, 12
N_OWN = 64
MESH = pl.DeviceIdType.MESH
F32 = jnp.float32
BF16 = jnp.bfloat16
CLASSES = ((0, 64), (64, 128), (192, 256), (448, 512))
BLOCKS = ((0, 1), (1, 1), (2, 2), (4, 4))


I16 = jnp.int16
X_ORDER = (2, 1, 3)
Y_ORDER = (4, 3, 5, 2, 6, 1, 7)
BOTH = (("y", 4), ("y", 3), ("x", 2), ("y", 5), ("y", 2), ("x", 1), ("y", 6), ("y", 1), ("x", 3), ("y", 7))


def pack(tiles, q):
    top = jnp.abs(tiles[0])
    for tile in tiles[1:]:
        top = jnp.maximum(top, jnp.abs(tile))
    power = jnp.ceil(jnp.log2(jnp.maximum(top, 1e-30) * 1.001))
    scale = jnp.exp2(15.0 - power)
    for k, tile in enumerate(tiles):
        q[k] = jnp.round(tile * scale).astype(jnp.int32).astype(I16)
    q[len(tiles)] = power.astype(jnp.int32).astype(I16)


def unpack(q, number):
    scale = jnp.exp2(q[number].astype(jnp.int32).astype(F32) - 15.0)
    return [q[k].astype(jnp.int32).astype(F32) * scale for k in range(number)]


def tiles_of(value):
    return [
        value[r : r + 16, c : c + 128]
        for r in range(0, value.shape[0], 16)
        for c in range(0, value.shape[1], 128)
    ]


def kernel(
    scale,
    ups, pooled, proj, emb, state, looks, sizes,
    rows_out, state_out, pg_out,
    ups_v, pooled_v, proj_v, emb_v, state_v, looks_v, sizes_v,
    acc, sib, x1s, x1r, y1s, y1r, y2s, y2r, x2s, x2r, z1, z2, ga, gb, gx, gy,
    wide, uc_v, stage, abuf, arecv, tal,
    in_sem, sib_s, sib_r, x1_s, x1_r, y1_s, y1_r, y2_s, y2_r, x2_s, x2_r, z1_s, z1_r, z2_s, z2_r,
    a_s, a_r, ga_s, ga_r, gb_s, gb_r, gx_s, gx_r, gy_s, gy_r, hx_s, hx_r, hy_s, hy_r,
):
    g = lax.axis_index("grp")
    p = lax.axis_index("own")
    core = lax.rem(p, 2)
    xi = lax.rem(p // 2, NX)
    yi = p // (2 * NX)
    zq = g // 4
    zi = lax.rem(g, 4)
    other = 1 - core

    def at(y, x, c):
        return (g, (y * NX + x) * 2 + c)

    def remote(src, dst, send, recv, dev):
        return pltpu.make_async_remote_copy(
            src_ref=src, dst_ref=dst, send_sem=send, recv_sem=recv,
            device_id=dev, device_id_type=MESH,
        )

    ins = (
        (ups, ups_v), (pooled, pooled_v), (proj, proj_v), (looks, looks_v), (sizes, sizes_v), (emb, emb_v), (state, state_v),
    )
    loads = [pltpu.make_async_copy(a, b, in_sem.at[i]) for i, (a, b) in enumerate(ins)]
    for load in loads:
        load.start()

    barrier = pltpu.get_barrier_semaphore()

    @pl.loop(1, N_OWN)
    def _(i):
        pl.semaphore_signal(barrier, inc=1, device_id=(g, lax.rem(p + i, N_OWN)), device_id_type=MESH)

    def z_near(i):
        return (zq * 4 + lax.rem(zi + i, 4), p)

    def z_far(i):
        return (lax.rem(g + 4 * i, NZ), p)

    for i in (1, 2, 3):
        pl.semaphore_signal(barrier, inc=1, device_id=z_near(i), device_id_type=MESH)
    for i in (1, 2):
        pl.semaphore_signal(barrier, inc=1, device_id=z_far(i), device_id_type=MESH)

    for load in loads[:1]:
        load.wait()

    @pl.loop(0, 8)
    def _(b):
        some = ups_v[pl.ds(b * 32, 32)].astype(F32)
        for t in range(4):
            wide[t, pl.ds(pl.multiple_of(b * 128, 128), 128), :] = some[:, :, t * 128 : t * 128 + 128].reshape(128, 128)

    for c in range(4):
        for t in range(4):
            uc_v[c, :, t * 128 : t * 128 + 128] = wide[t, pl.ds(c, GB, stride=4), :].astype(BF16)

    loads[1].wait()

    def term(lo, hi, c):
        return lax.dot_general(
            pooled_v[:, lo:hi], uc_v[c], (((0,), (0,)), ((), ())), preferred_element_type=F32
        )

    def keep(half, row, value):
        for part in range(2):
            acc[half, part, row : row + value.shape[0], :] = value[:, part * 256 : part * 256 + 256]

    keep(0, 0, term(384, 960, 3)[64:576])
    keep(1, 0, term(0, 128, 0))
    keep(1, 128, term(0, 256, 1)[64:192])
    keep(1, 256, term(128, 512, 2)[64:320])

    pl.semaphore_wait(barrier, N_OWN - 1 + 5)

    def span(kind, i):
        if kind == "x":
            t = lax.rem(xi + i, NX)
            return t, pl.ds(pl.multiple_of(t * 128, 128), 128)
        t = lax.rem(yi + i, NY)
        return t, pl.ds(pl.multiple_of(t * 64, 64), 64)

    def part_of(kind):
        return 0 if kind == "x" else 1

    sib_dev = at(yi, xi, other)
    steps = BOTH + (("x", 0), ("y", 0))
    sib_copies = {}
    for n, (kind, i) in enumerate(steps):
        t, rows = span(kind, i)
        part = part_of(kind)
        copy = remote(acc.at[other, part, rows], sib.at[part, rows], sib_s.at[n], sib_r.at[n], sib_dev)
        copy.start()
        sib_copies[kind, i] = copy

    def chip_sum(kind, i):
        t, rows = span(kind, i)
        part = part_of(kind)
        return acc[core, part, rows, :] + sib[part, rows, :]

    first = {}
    for kind, i in BOTH:
        sib_copies[kind, i].wait_recv()
        t, rows = span(kind, i)
        if kind == "x":
            pack(tiles_of(chip_sum(kind, i)), x1s.at[i - 1])
            copy = remote(x1s.at[i - 1], x1r.at[i - 1], x1_s.at[i - 1], x1_r.at[i - 1], at(yi, t, core))
        else:
            pack(tiles_of(chip_sum(kind, i)), y1s.at[i - 1])
            copy = remote(y1s.at[i - 1], y1r.at[i - 1], y1_s.at[i - 1], y1_r.at[i - 1], at(t, xi, core))
        copy.start()
        first[kind, i] = copy

    loads[2].wait()
    for c, ((offset, width), (block, number)) in enumerate(zip(CLASSES, BLOCKS)):
        bag = lax.dot_general(
            uc_v[c], proj_v[offset : offset + number * 128], (((1,), (1,)), ((), ())),
            preferred_element_type=F32,
        )
        for k in range(number):
            for s in range(4):
                stage[pl.ds(s * 8 + block + k, N_OWN, stride=32), :] = bag[
                    s * 64 : s * 64 + 64, k * 128 : k * 128 + 128
                ]
    abuf[...] = stage[...].reshape(N_OWN, 32, 128).astype(BF16)

    loads[3].wait()
    loads[4].wait()
    spread = lax.broadcasted_iota(jnp.int32, (GB, GB), 0)
    order = (spread & 63) * 4 + (spread >> 6)
    picked = jnp.where(order == lax.broadcasted_iota(jnp.int32, (GB, GB), 1), 1.0, 0.0).astype(BF16)
    for member in range(4):
        valid = lax.broadcasted_iota(jnp.int32, (BAG, GB), 0) < sizes_v[member : member + 1, :]
        wanted = jnp.where(valid, looks_v[member], -1)
        parts = []
        for r in range(0, GB, 64):
            ids = lax.broadcasted_iota(jnp.int32, (64, GB), 0) + r
            count = jnp.zeros((64, GB), F32)
            for l in range(BAG):
                count += jnp.where(wanted[l : l + 1, :] == ids, 1.0, 0.0)
            parts.append(count.astype(BF16))
        counts = jnp.concatenate(parts, axis=0)
        tal[member] = lax.dot_general(
            picked, counts, (((1,), (1,)), ((), ())), preferred_element_type=F32
        ).astype(BF16)

    second = {}
    sib_copies["x", 0].wait_recv()
    total = tiles_of(chip_sum("x", 0))
    for i in X_ORDER:
        first["x", i].wait_recv()
        total = [a + b for a, b in zip(total, unpack(x1r.at[i - 1], 16))]
    for k, tile in enumerate(total):
        y2s[k // 2, :, (k % 2) * 128 : (k % 2) * 128 + 128] = tile
    for i in Y_ORDER:
        t, rows = span("y", i)
        copy = remote(y2s.at[t], y2r.at[i - 1], y2_s.at[i - 1], y2_r.at[i - 1], at(t, xi, core))
        copy.start()
        second["y", i] = copy
    sib_copies["y", 0].wait_recv()
    total = tiles_of(chip_sum("y", 0))
    for i in Y_ORDER:
        first["y", i].wait_recv()
        total = [a + b for a, b in zip(total, unpack(y1r.at[i - 1], 8))]
    for k, tile in enumerate(total):
        x2s[k // 2, :, (k % 2) * 128 : (k % 2) * 128 + 128] = tile
    for i in X_ORDER:
        t, rows = span("x", i)
        copy = remote(x2s.at[t], x2r.at[i - 1], x2_s.at[i - 1], x2_r.at[i - 1], at(yi, t, core))
        copy.start()
        second["x", i] = copy

    def to_owner(i):
        t = lax.rem(p + i, N_OWN)
        return remote(abuf.at[t], arecv.at[p], a_s, a_r, (g, t))

    @pl.loop(1, N_OWN)
    def _(i):
        to_owner(i).start()

    arecv[p] = abuf[p]

    part = y2s[yi]
    for i in Y_ORDER:
        second["y", i].wait_recv()
        part += y2r[i - 1]
    z1[zi, :, 0:256] = part
    part = x2s[xi]
    for i in X_ORDER:
        second["x", i].wait_recv()
        part += x2r[i - 1]
    z1[zi, :, 256:512] = part

    z1_copies = []
    for i in (1, 2, 3):
        copy = remote(z1.at[zi], z1.at[zi], z1_s.at[i - 1], z1_r.at[i - 1], z_near(i))
        copy.start()
        z1_copies.append(copy)
    for copy in z1_copies:
        copy.wait_recv()
    z2[zq] = (z1[0] + z1[1]) + (z1[2] + z1[3])
    z2_copies = []
    for i in (1, 2):
        copy = remote(z2.at[zq], z2.at[zq], z2_s.at[i - 1], z2_r.at[i - 1], z_far(i))
        copy.start()
        z2_copies.append(copy)
    for copy in z2_copies:
        copy.wait_recv()
    whole = ((z2[0] + z2[1]) + z2[2]) * scale

    ga[yi] = whole[:, 0:256]
    gb[xi] = whole[:, 256:512]
    back = {}
    for i in X_ORDER:
        t, rows = span("x", i)
        back["x", i] = remote(gb.at[xi], gb.at[xi], gb_s.at[i - 1], gb_r.at[i - 1], at(yi, t, core))
        back["x", i].start()
    for i in Y_ORDER:
        t, rows = span("y", i)
        back["y", i] = remote(ga.at[yi], ga.at[yi], ga_s.at[i - 1], ga_r.at[i - 1], at(t, xi, core))
        back["y", i].start()

    pltpu.make_async_copy(arecv.at[pl.ds(0, N_OWN - 1)], arecv.at[pl.ds(0, N_OWN - 1)], a_r).wait()
    loads[5].wait()
    loads[6].wait()
    stage[...] = arecv[...].astype(F32).reshape(N_OWN * 32, 128)
    for member, ((offset, width), (block, number)) in enumerate(zip(CLASSES, BLOCKS)):
        columns = []
        for k in range(number):
            columns.append(
                jnp.concatenate(
                    [stage[pl.ds(s * 8 + block + k, N_OWN, stride=32), :] for s in range(4)], axis=0
                ).astype(BF16)
            )
        bags = columns[0] if number == 1 else jnp.concatenate(columns, axis=1)
        grad = lax.dot_general(
            bags, tal[member], (((0,), (0,)), ((), ())), preferred_element_type=F32
        )[:width]
        new = state_v[member : member + 1, :] + jnp.sum(grad * grad, axis=0, keepdims=True) * (1.0 / width)
        state_out[member : member + 1, :] = new
        rows_out[offset : offset + width, :] = emb_v[offset : offset + width, :] - grad * (LEARN / jnp.sqrt(new))
    last = {}
    hand = {}

    def slot(kind, half, t):
        return gx.at[half, t] if kind == "x" else gy.at[half, t]

    def to_other(kind, i, t):
        sems = (hx_s.at[i], hx_r.at[i]) if kind == "x" else (hy_s.at[i], hy_r.at[i])
        hand[kind, i] = remote(slot(kind, core, t), slot(kind, core, t), *sems, sib_dev)
        hand[kind, i].start()

    def put(kind, half, t):
        top = (1 - half) * 32
        number, left = (16, 0) if kind == "x" else (8, 256)
        for k, tile in enumerate(unpack(slot(kind, half, t), number)):
            column = left + (k % 2) * 128
            pg_out[top + t * (number // 2) + k // 2, :, column : column + 128] = tile

    def spread_out(kind, i):
        t, rows = span(kind, i)
        if kind == "x":
            sems, dev = (gx_s.at[i - 1], gx_r.at[i - 1]), at(yi, t, core)
            mine = slot("x", core, xi)
        else:
            sems, dev = (gy_s.at[i - 1], gy_r.at[i - 1]), at(t, xi, core)
            mine = slot("y", core, yi)
        last[kind, i] = remote(mine, mine, *sems, dev)
        last[kind, i].start()

    for i in X_ORDER:
        back["x", i].wait_recv()
    pack([gb[k // 2, :, (k % 2) * 128 : (k % 2) * 128 + 128] for k in range(8)], slot("y", core, yi))
    for i in Y_ORDER:
        spread_out("y", i)
    to_other("y", 0, yi)
    for i in Y_ORDER:
        back["y", i].wait_recv()
    pack([ga[k // 2, :, (k % 2) * 128 : (k % 2) * 128 + 128] for k in range(16)], slot("x", core, xi))
    for i in X_ORDER:
        spread_out("x", i)
    to_other("x", 0, xi)
    put("y", core, yi)
    put("x", core, xi)
    for kind, i in BOTH:
        last[kind, i].wait_recv()
        t = lax.rem(xi - i + NX, NX) if kind == "x" else lax.rem(yi - i + NY, NY)
        to_other(kind, i, t)
        put(kind, core, t)
    for kind, i in (("y", 0), ("x", 0)) + BOTH:
        hand[kind, i].wait_recv()
        t = lax.rem(xi - i + NX, NX) if kind == "x" else lax.rem(yi - i + NY, NY)
        put(kind, other, t)

    for group in (sib_copies, first, second, back, last, hand):
        for copy in group.values():
            copy.wait_send()
    for copy in z1_copies + z2_copies:
        copy.wait_send()

    @pl.loop(1, N_OWN)
    def _(i):
        to_owner(i).wait_send()


def on_device(upstream, pooled, projection, embedding, row_state, lookups, bag_sizes):
    total_bags = upstream.shape[0] * lax.axis_size("grp") * lax.axis_size("own") * upstream.shape[1]
    scale = 1.0 / math.sqrt(total_bags)
    operands = (
        upstream.reshape(GB, 4, 512), pooled.reshape(GB, 960), projection, embedding.T, row_state,
        jnp.transpose(lookups[0], (0, 2, 1)), bag_sizes[0],
    )
    dma = pltpu.SemaphoreType.DMA
    any_space = pl.BlockSpec(memory_space=pl.ANY)
    scratch = [pltpu.VMEM(a.shape, a.dtype) for a in operands] + [
        pltpu.VMEM((2, 2, 512, 256), F32),
        pltpu.VMEM((2, 512, 256), F32),
        pltpu.VMEM((3, 17, 16, 128), I16),
        pltpu.VMEM((3, 17, 16, 128), I16),
        pltpu.VMEM((7, 9, 16, 128), I16),
        pltpu.VMEM((7, 9, 16, 128), I16),
        pltpu.VMEM((8, 16, 256), F32),
        pltpu.VMEM((7, 16, 256), F32),
        pltpu.VMEM((4, 16, 256), F32),
        pltpu.VMEM((3, 16, 256), F32),
        pltpu.VMEM((4, 16, 512), F32),
        pltpu.VMEM((3, 16, 512), F32),
        pltpu.VMEM((8, 16, 256), F32),
        pltpu.VMEM((4, 16, 256), F32),
        pltpu.VMEM((2, 4, 17, 16, 128), I16),
        pltpu.VMEM((2, 8, 9, 16, 128), I16),
        pltpu.VMEM((4, 4 * GB, 128), F32),
        pltpu.VMEM((4, GB, 512), BF16),
        pltpu.VMEM((N_OWN * 32, 128), F32),
        pltpu.VMEM((N_OWN, 32, 128), BF16),
        pltpu.VMEM((N_OWN, 32, 128), BF16),
        pltpu.VMEM((4, GB, GB), BF16),
    ] + [
        dma(() if n == 0 else (n,))
        for n in (7, 12, 12, 3, 3, 7, 7, 7, 7, 3, 3, 3, 3, 2, 2, 0, 0, 7, 7, 3, 3, 3, 3, 7, 7, 4, 4, 8, 8)
    ]
    rows_t, new_state, pg = pl.pallas_call(
        functools.partial(kernel, scale),
        out_shape=(
            pltpu.VMEM((960, GB), F32),
            pltpu.VMEM((4, GB), F32),
            pltpu.VMEM((64, 16, 512), F32),
        ),
        in_specs=[pl.BlockSpec(memory_space=pltpu.HBM)] * len(operands),
        out_specs=(pl.BlockSpec(memory_space=pltpu.VMEM),) * 3,
        scratch_shapes=scratch,
        compiler_params=pltpu.CompilerParams(
            collective_id=0, has_side_effects=True, vmem_limit_bytes=54 * 2**20
        ),
        name="fused",
    )(*operands)
    pg = jnp.concatenate([pg[0:4], pg[8:64]], axis=0).reshape(960, 512)
    return rows_t.T, new_state, pg


def solution(mesh):
    return jax.shard_map(
        on_device,
        mesh=mesh,
        in_specs=(
            P(("grp", "own"), None, None, None),
            P(("grp", "own"), None, None),
            P(),
            P(("grp", "own"), None),
            P(None, ("grp", "own")),
            P(("grp", "own"), None, None, None),
            P(("grp", "own"), None, None),
        ),
        out_specs=(P(("grp", "own"), None), P(None, ("grp", "own")), P()),
        check_vma=False,
    )
```

```python
import functools
import math

import jax
import jax.numpy as jnp
from jax import lax
from jax.experimental import pallas as pl
from jax.experimental.pallas import tpu as pltpu
from jax.sharding import PartitionSpec as P

BAG = 16
GB = 256
LEARN = 0.05
NX, NY, NZ = 4, 8, 12
N_OWN = 64
MESH = pl.DeviceIdType.MESH
F32 = jnp.float32
BF16 = jnp.bfloat16
CLASSES = ((0, 64), (64, 128), (192, 256), (448, 512))
BLOCKS = ((0, 1), (1, 1), (2, 2), (4, 4))


I16 = jnp.int16
X_ORDER = (2, 1, 3)
Y_ORDER = (4, 3, 5, 2, 6, 1, 7)
BOTH = (("y", 4), ("y", 3), ("x", 2), ("y", 5), ("y", 2), ("x", 1), ("y", 6), ("y", 1), ("x", 3), ("y", 7))


def pack(tiles, q):
    top = jnp.abs(tiles[0])
    for tile in tiles[1:]:
        top = jnp.maximum(top, jnp.abs(tile))
    power = jnp.ceil(jnp.log2(jnp.maximum(top, 1e-30) * 1.001))
    scale = jnp.exp2(15.0 - power)
    for k, tile in enumerate(tiles):
        q[k] = jnp.round(tile * scale).astype(jnp.int32).astype(I16)
    q[len(tiles)] = power.astype(jnp.int32).astype(I16)


def unpack(q, number):
    scale = jnp.exp2(q[number].astype(jnp.int32).astype(F32) - 15.0)
    return [q[k].astype(jnp.int32).astype(F32) * scale for k in range(number)]


def tiles_of(value):
    return [
        value[r : r + 16, c : c + 128]
        for r in range(0, value.shape[0], 16)
        for c in range(0, value.shape[1], 128)
    ]


def kernel(
    scale,
    ups, pooled, proj, emb, state, looks, sizes,
    rows_out, state_out, pg_out,
    ups_v, pooled_v, proj_v, emb_v, state_v, looks_v, sizes_v,
    acc, sib, x1s, x1r, y1s, y1r, y2s, y2r, x2s, x2r, z1, z2, ga, gb, gx, gy,
    wide, uc_v, stage, abuf, arecv, tal,
    in_sem, sib_s, sib_r, x1_s, x1_r, y1_s, y1_r, y2_s, y2_r, x2_s, x2_r, z1_s, z1_r, z2_s, z2_r,
    a_s, a_r, ga_s, ga_r, gb_s, gb_r, gx_s, gx_r, gy_s, gy_r, hx_s, hx_r, hy_s, hy_r,
):
    g = lax.axis_index("grp")
    p = lax.axis_index("own")
    core = lax.rem(p, 2)
    xi = lax.rem(p // 2, NX)
    yi = p // (2 * NX)
    zq = g // 4
    zi = lax.rem(g, 4)
    other = 1 - core

    def at(y, x, c):
        return (g, (y * NX + x) * 2 + c)

    def remote(src, dst, send, recv, dev):
        return pltpu.make_async_remote_copy(
            src_ref=src, dst_ref=dst, send_sem=send, recv_sem=recv,
            device_id=dev, device_id_type=MESH,
        )

    ins = (
        (ups, ups_v), (pooled, pooled_v), (proj, proj_v), (looks, looks_v), (sizes, sizes_v), (emb, emb_v), (state, state_v),
    )
    barrier = pltpu.get_barrier_semaphore()

    def z_near(i):
        return (zq * 4 + lax.rem(zi + i, 4), p)

    def z_far(i):
        return (lax.rem(g + 4 * i, NZ), p)

    partners = (
        [at(lax.rem(yi + i, NY), xi, core) for i in Y_ORDER]
        + [at(yi, lax.rem(xi + i, NX), core) for i in X_ORDER]
        + [at(yi, xi, other)]
        + [z_far(i) for i in (1, 2)]
        + [z_near(i) for i in (2, 1, 3)]
    )
    for dev in partners:
        pl.semaphore_signal(barrier, inc=1, device_id=dev, device_id_type=MESH)

    loads = [pltpu.make_async_copy(a, b, in_sem.at[i]) for i, (a, b) in enumerate(ins)]
    for load in loads:
        load.start()

    for load in loads[:1]:
        load.wait()

    @pl.loop(0, 8)
    def _(b):
        some = ups_v[pl.ds(b * 32, 32)].astype(F32)
        for t in range(4):
            wide[t, pl.ds(pl.multiple_of(b * 128, 128), 128), :] = some[:, :, t * 128 : t * 128 + 128].reshape(128, 128)

    for c in range(4):
        for t in range(4):
            uc_v[c, :, t * 128 : t * 128 + 128] = wide[t, pl.ds(c, GB, stride=4), :].astype(BF16)

    loads[1].wait()

    def term(lo, hi, c):
        return lax.dot_general(
            pooled_v[:, lo:hi], uc_v[c], (((0,), (0,)), ((), ())), preferred_element_type=F32
        )

    def keep(half, row, value):
        for part in range(2):
            acc[half, part, row : row + value.shape[0], :] = value[:, part * 256 : part * 256 + 256]

    keep(0, 0, term(384, 960, 3)[64:576])
    keep(1, 0, term(0, 128, 0))
    keep(1, 128, term(0, 256, 1)[64:192])
    keep(1, 256, term(128, 512, 2)[64:320])

    pl.semaphore_wait(barrier, len(partners))

    def span(kind, i):
        if kind == "x":
            t = lax.rem(xi + i, NX)
            return t, pl.ds(pl.multiple_of(t * 128, 128), 128)
        t = lax.rem(yi + i, NY)
        return t, pl.ds(pl.multiple_of(t * 64, 64), 64)

    def part_of(kind):
        return 0 if kind == "x" else 1

    sib_dev = at(yi, xi, other)
    steps = BOTH + (("x", 0), ("y", 0))
    sib_copies = {}
    for n, (kind, i) in enumerate(steps):
        t, rows = span(kind, i)
        part = part_of(kind)
        copy = remote(acc.at[other, part, rows], sib.at[part, rows], sib_s.at[n], sib_r.at[n], sib_dev)
        copy.start()
        sib_copies[kind, i] = copy

    def chip_sum(kind, i):
        t, rows = span(kind, i)
        part = part_of(kind)
        return acc[core, part, rows, :] + sib[part, rows, :]

    first = {}
    for kind, i in BOTH:
        sib_copies[kind, i].wait_recv()
        t, rows = span(kind, i)
        if kind == "x":
            pack(tiles_of(chip_sum(kind, i)), x1s.at[i - 1])
            copy = remote(x1s.at[i - 1], x1r.at[i - 1], x1_s.at[i - 1], x1_r.at[i - 1], at(yi, t, core))
        else:
            pack(tiles_of(chip_sum(kind, i)), y1s.at[i - 1])
            copy = remote(y1s.at[i - 1], y1r.at[i - 1], y1_s.at[i - 1], y1_r.at[i - 1], at(t, xi, core))
        copy.start()
        first[kind, i] = copy

    loads[2].wait()
    for c, ((offset, width), (block, number)) in enumerate(zip(CLASSES, BLOCKS)):
        bag = lax.dot_general(
            uc_v[c], proj_v[offset : offset + number * 128], (((1,), (1,)), ((), ())),
            preferred_element_type=F32,
        )
        for k in range(number):
            for s in range(4):
                stage[pl.ds(s * 8 + block + k, N_OWN, stride=32), :] = bag[
                    s * 64 : s * 64 + 64, k * 128 : k * 128 + 128
                ]
    abuf[...] = stage[...].reshape(N_OWN, 32, 128).astype(BF16)

    loads[3].wait()
    loads[4].wait()
    spread = lax.broadcasted_iota(jnp.int32, (GB, GB), 0)
    order = (spread & 63) * 4 + (spread >> 6)
    picked = jnp.where(order == lax.broadcasted_iota(jnp.int32, (GB, GB), 1), 1.0, 0.0).astype(BF16)
    for member in range(4):
        valid = lax.broadcasted_iota(jnp.int32, (BAG, GB), 0) < sizes_v[member : member + 1, :]
        wanted = jnp.where(valid, looks_v[member], -1)
        parts = []
        for r in range(0, GB, 64):
            ids = lax.broadcasted_iota(jnp.int32, (64, GB), 0) + r
            count = jnp.zeros((64, GB), F32)
            for l in range(BAG):
                count += jnp.where(wanted[l : l + 1, :] == ids, 1.0, 0.0)
            parts.append(count.astype(BF16))
        counts = jnp.concatenate(parts, axis=0)
        tal[member] = lax.dot_general(
            picked, counts, (((1,), (1,)), ((), ())), preferred_element_type=F32
        ).astype(BF16)

    second = {}
    sib_copies["x", 0].wait_recv()
    total = tiles_of(chip_sum("x", 0))
    for i in X_ORDER:
        first["x", i].wait_recv()
        total = [a + b for a, b in zip(total, unpack(x1r.at[i - 1], 16))]
    for k, tile in enumerate(total):
        y2s[k // 2, :, (k % 2) * 128 : (k % 2) * 128 + 128] = tile
    for i in Y_ORDER:
        t, rows = span("y", i)
        copy = remote(y2s.at[t], y2r.at[i - 1], y2_s.at[i - 1], y2_r.at[i - 1], at(t, xi, core))
        copy.start()
        second["y", i] = copy
    sib_copies["y", 0].wait_recv()
    total = tiles_of(chip_sum("y", 0))
    for i in Y_ORDER:
        first["y", i].wait_recv()
        total = [a + b for a, b in zip(total, unpack(y1r.at[i - 1], 8))]
    for k, tile in enumerate(total):
        x2s[k // 2, :, (k % 2) * 128 : (k % 2) * 128 + 128] = tile
    for i in X_ORDER:
        t, rows = span("x", i)
        copy = remote(x2s.at[t], x2r.at[i - 1], x2_s.at[i - 1], x2_r.at[i - 1], at(yi, t, core))
        copy.start()
        second["x", i] = copy

    def near(n, mine):
        copies = []
        z1[n, zi] = mine
        for i in (3, 2, 1):
            slot = z1.at[n, zi]
            copies.append(remote(slot, slot, z1_s.at[n, i - 1], z1_r.at[n, i - 1], z_near(i)))
            copies[-1].start()
        return copies

    def far(n):
        copies = []
        z2[n, zq] = (z1[n, 0] + z1[n, 1]) + (z1[n, 2] + z1[n, 3])
        for i in (1, 2):
            slot = z2.at[n, zq]
            copies.append(remote(slot, slot, z2_s.at[n, i - 1], z2_r.at[n, i - 1], z_far(i)))
            copies[-1].start()
        return copies

    def to_owner(i):
        t = lax.rem(p + i, N_OWN)
        return remote(abuf.at[t], arecv.at[p], a_s, a_r, (g, t))

    def send_bags():
        @pl.loop(1, N_OWN)
        def _(i):
            to_owner(i).start()

        arecv[p] = abuf[p]

    z_copies = []
    waiting = []
    for n, (order, kind, own, got) in enumerate(((Y_ORDER, "y", y2s, y2r), (X_ORDER, "x", x2s, x2r))):
        part = own[yi if kind == "y" else xi]
        for i in order:
            second[kind, i].wait_recv()
            part += got[i - 1]
        waiting.append(near(n, part))
        z_copies += waiting[-1]
        if n == 0:
            send_bags()

    for n in range(2):
        for copy in waiting[n]:
            copy.wait_recv()
        waiting[n] = far(n)
        z_copies += waiting[n]

    back = {}
    for n, (order, kind, gathered) in enumerate(((Y_ORDER, "y", ga), (X_ORDER, "x", gb))):
        for copy in waiting[n]:
            copy.wait_recv()
        here = yi if kind == "y" else xi
        gathered[here] = ((z2[n, 0] + z2[n, 1]) + z2[n, 2]) * scale
        for i in order:
            t, rows = span(kind, i)
            if kind == "y":
                sems, dev = (ga_s.at[i - 1], ga_r.at[i - 1]), at(t, xi, core)
            else:
                sems, dev = (gb_s.at[i - 1], gb_r.at[i - 1]), at(yi, t, core)
            back[kind, i] = remote(gathered.at[here], gathered.at[here], *sems, dev)
            back[kind, i].start()

    last = {}
    hand = {}

    def slot(kind, half, t):
        return gx.at[half, t] if kind == "x" else gy.at[half, t]

    def to_other(kind, i, t):
        sems = (hx_s.at[i], hx_r.at[i]) if kind == "x" else (hy_s.at[i], hy_r.at[i])
        hand[kind, i] = remote(slot(kind, core, t), slot(kind, core, t), *sems, sib_dev)
        hand[kind, i].start()

    def put(kind, half, t):
        number, left, groups = (16, 0, 8) if kind == "x" else (8, 256, 4)
        later = (t + 7) // 8 if kind == "y" else (t + 3) // 4
        for k, tile in enumerate(unpack(slot(kind, half, t), number)):
            column = left + (k % 2) * 128
            r = k // 2
            plain = t * groups + r
            if kind == "x":
                moved = plain - 4 * later + (0 if r < 4 else 56 * (1 - later))
            else:
                moved = plain - 4 * later + 60 * (later - (t + 6) // 8)
            row = half * moved + (1 - half) * (plain + 28)
            pg_out[row, :, column : column + 128] = tile

    def spread_out(kind, i):
        t, rows = span(kind, i)
        if kind == "x":
            sems, dev = (gx_s.at[i - 1], gx_r.at[i - 1]), at(yi, t, core)
            mine = slot("x", core, xi)
        else:
            sems, dev = (gy_s.at[i - 1], gy_r.at[i - 1]), at(t, xi, core)
            mine = slot("y", core, yi)
        last[kind, i] = remote(mine, mine, *sems, dev)
        last[kind, i].start()

    for i in X_ORDER:
        back["x", i].wait_recv()
    pack([gb[k // 2, :, (k % 2) * 128 : (k % 2) * 128 + 128] for k in range(8)], slot("y", core, yi))
    for i in Y_ORDER:
        spread_out("y", i)
    to_other("y", 0, yi)
    for i in Y_ORDER:
        back["y", i].wait_recv()
    pack([ga[k // 2, :, (k % 2) * 128 : (k % 2) * 128 + 128] for k in range(16)], slot("x", core, xi))
    for i in X_ORDER:
        spread_out("x", i)
    to_other("x", 0, xi)
    pltpu.make_async_copy(arecv.at[pl.ds(0, N_OWN - 1)], arecv.at[pl.ds(0, N_OWN - 1)], a_r).wait()
    loads[5].wait()
    loads[6].wait()
    stage[...] = arecv[...].astype(F32).reshape(N_OWN * 32, 128)
    for member, ((offset, width), (block, number)) in enumerate(zip(CLASSES, BLOCKS)):
        columns = []
        for k in range(number):
            columns.append(
                jnp.concatenate(
                    [stage[pl.ds(s * 8 + block + k, N_OWN, stride=32), :] for s in range(4)], axis=0
                ).astype(BF16)
            )
        bags = columns[0] if number == 1 else jnp.concatenate(columns, axis=1)
        grad = lax.dot_general(
            bags, tal[member], (((0,), (0,)), ((), ())), preferred_element_type=F32
        )[:width]
        new = state_v[member : member + 1, :] + jnp.sum(grad * grad, axis=0, keepdims=True) * (1.0 / width)
        state_out[member : member + 1, :] = new
        rows_out[offset : offset + width, :] = emb_v[offset : offset + width, :] - grad * (LEARN / jnp.sqrt(new))
    put("y", core, yi)
    put("x", core, xi)
    for kind, i in BOTH:
        last[kind, i].wait_recv()
        t = lax.rem(xi - i + NX, NX) if kind == "x" else lax.rem(yi - i + NY, NY)
        to_other(kind, i, t)
        put(kind, core, t)
    for kind, i in (("y", 0), ("x", 0)) + BOTH:
        hand[kind, i].wait_recv()
        t = lax.rem(xi - i + NX, NX) if kind == "x" else lax.rem(yi - i + NY, NY)
        put(kind, other, t)

    for group in (sib_copies, first, second, back, last, hand):
        for copy in group.values():
            copy.wait_send()
    for copy in z_copies:
        copy.wait_send()

    @pl.loop(1, N_OWN)
    def _(i):
        to_owner(i).wait_send()


def on_device(upstream, pooled, projection, embedding, row_state, lookups, bag_sizes):
    total_bags = upstream.shape[0] * lax.axis_size("grp") * lax.axis_size("own") * upstream.shape[1]
    scale = 1.0 / math.sqrt(total_bags)
    operands = (
        upstream.reshape(GB, 4, 512), pooled.reshape(GB, 960), projection, embedding.T, row_state,
        jnp.transpose(lookups[0], (0, 2, 1)), bag_sizes[0],
    )
    dma = pltpu.SemaphoreType.DMA
    any_space = pl.BlockSpec(memory_space=pl.ANY)
    scratch = [pltpu.VMEM(a.shape, a.dtype) for a in operands] + [
        pltpu.VMEM((2, 2, 512, 256), F32),
        pltpu.VMEM((2, 512, 256), F32),
        pltpu.VMEM((3, 17, 16, 128), I16),
        pltpu.VMEM((3, 17, 16, 128), I16),
        pltpu.VMEM((7, 9, 16, 128), I16),
        pltpu.VMEM((7, 9, 16, 128), I16),
        pltpu.VMEM((8, 16, 256), F32),
        pltpu.VMEM((7, 16, 256), F32),
        pltpu.VMEM((4, 16, 256), F32),
        pltpu.VMEM((3, 16, 256), F32),
        pltpu.VMEM((2, 4, 16, 256), F32),
        pltpu.VMEM((2, 3, 16, 256), F32),
        pltpu.VMEM((8, 16, 256), F32),
        pltpu.VMEM((4, 16, 256), F32),
        pltpu.VMEM((2, 4, 17, 16, 128), I16),
        pltpu.VMEM((2, 8, 9, 16, 128), I16),
        pltpu.VMEM((4, 4 * GB, 128), F32),
        pltpu.VMEM((4, GB, 512), BF16),
        pltpu.VMEM((N_OWN * 32, 128), F32),
        pltpu.VMEM((N_OWN, 32, 128), BF16),
        pltpu.VMEM((N_OWN, 32, 128), BF16),
        pltpu.VMEM((4, GB, GB), BF16),
    ] + [
        dma(n if isinstance(n, tuple) else () if n == 0 else (n,))
        for n in (7, 12, 12, 3, 3, 7, 7, 7, 7, 3, 3, (2, 3), (2, 3), (2, 2), (2, 2), 0, 0, 7, 7, 3, 3, 3, 3, 7, 7, 4, 4, 8, 8)
    ]
    rows_t, new_state, pg = pl.pallas_call(
        functools.partial(kernel, scale),
        out_shape=(
            pltpu.VMEM((960, GB), F32),
            pltpu.VMEM((4, GB), F32),
            pltpu.VMEM((64, 16, 512), F32),
        ),
        in_specs=[pl.BlockSpec(memory_space=pltpu.HBM)] * len(operands),
        out_specs=(pl.BlockSpec(memory_space=pltpu.VMEM),) * 3,
        scratch_shapes=scratch,
        compiler_params=pltpu.CompilerParams(
            collective_id=0, has_side_effects=True, vmem_limit_bytes=54 * 2**20
        ),
        name="fused",
    )(*operands)
    return rows_t.T, new_state, pg[0:60].reshape(960, 512)


def solution(mesh):
    return jax.shard_map(
        on_device,
        mesh=mesh,
        in_specs=(
            P(("grp", "own"), None, None, None),
            P(("grp", "own"), None, None),
            P(),
            P(("grp", "own"), None),
            P(None, ("grp", "own")),
            P(("grp", "own"), None, None, None),
            P(("grp", "own"), None, None),
        ),
        out_specs=(P(("grp", "own"), None), P(None, ("grp", "own")), P()),
        check_vma=False,
    )
```

```python
import functools
import math

import jax
import jax.numpy as jnp
from jax import lax
from jax.experimental import pallas as pl
from jax.experimental.pallas import tpu as pltpu
from jax.sharding import PartitionSpec as P

BAG = 16
GB = 256
LEARN = 0.05
NX, NY, NZ = 4, 8, 12
N_OWN = 64
MESH = pl.DeviceIdType.MESH
F32 = jnp.float32
BF16 = jnp.bfloat16
CLASSES = ((0, 64), (64, 128), (192, 256), (448, 512))
BLOCKS = ((0, 1), (1, 1), (2, 2), (4, 4))


I16 = jnp.int16
X_ORDER = (2, 1, 3)
Y_ORDER = (4, 3, 5, 2, 6, 1, 7)
BOTH = (("y", 4), ("y", 3), ("y", 5), ("y", 2), ("x", 2), ("y", 6), ("y", 1), ("x", 1), ("y", 7), ("x", 3))


def pack(tiles, q):
    top = jnp.abs(tiles[0])
    for tile in tiles[1:]:
        top = jnp.maximum(top, jnp.abs(tile))
    power = jnp.ceil(jnp.log2(jnp.maximum(top, 1e-30) * 1.001))
    scale = jnp.exp2(15.0 - power)
    for k, tile in enumerate(tiles):
        q[k] = jnp.round(tile * scale).astype(jnp.int32).astype(I16)
    q[len(tiles)] = power.astype(jnp.int32).astype(I16)


def unpack(q, number):
    scale = jnp.exp2(q[number].astype(jnp.int32).astype(F32) - 15.0)
    return [q[k].astype(jnp.int32).astype(F32) * scale for k in range(number)]


def tiles_of(value):
    return [
        value[r : r + 16, c : c + 128]
        for r in range(0, value.shape[0], 16)
        for c in range(0, value.shape[1], 128)
    ]


def kernel(
    scale,
    ups, pooled, proj, emb, state, looks, sizes,
    rows_out, state_out, pg_out,
    ups_v, pooled_v, proj_v, emb_v, state_v, looks_v, sizes_v,
    acc, sib, x1s, x1r, y1s, y1r, y2s, y2r, x2s, x2r, z1, z2, ga, gb, gx, gy,
    wide, uc_v, stage, abuf, arecv, tal,
    in_sem, sib_s, sib_r, x1_s, x1_r, y1_s, y1_r, y2_s, y2_r, x2_s, x2_r, z1_s, z1_r, z2_s, z2_r,
    a_s, a_r, ga_s, ga_r, gb_s, gb_r, gx_s, gx_r, gy_s, gy_r, hx_s, hx_r, hy_s, hy_r,
):
    g = lax.axis_index("grp")
    p = lax.axis_index("own")
    core = lax.rem(p, 2)
    xi = lax.rem(p // 2, NX)
    yi = p // (2 * NX)
    zq = g // 4
    zi = lax.rem(g, 4)
    other = 1 - core

    def at(y, x, c):
        return (g, (y * NX + x) * 2 + c)

    def remote(src, dst, send, recv, dev):
        return pltpu.make_async_remote_copy(
            src_ref=src, dst_ref=dst, send_sem=send, recv_sem=recv,
            device_id=dev, device_id_type=MESH,
        )

    ins = (
        (ups, ups_v), (pooled, pooled_v), (proj, proj_v), (looks, looks_v), (sizes, sizes_v), (emb, emb_v), (state, state_v),
    )
    barrier = pltpu.get_barrier_semaphore()

    def z_near(i):
        return (zq * 4 + lax.rem(zi + i, 4), p)

    def z_far(i):
        return (lax.rem(g + 4 * i, NZ), p)

    partners = (
        [at(lax.rem(yi + i, NY), xi, core) for i in Y_ORDER]
        + [at(yi, lax.rem(xi + i, NX), core) for i in X_ORDER]
        + [at(yi, xi, other)]
        + [z_far(i) for i in (1, 2)]
        + [z_near(i) for i in (2, 1, 3)]
    )
    for dev in partners:
        pl.semaphore_signal(barrier, inc=1, device_id=dev, device_id_type=MESH)

    loads = [pltpu.make_async_copy(a, b, in_sem.at[i]) for i, (a, b) in enumerate(ins)]
    for load in loads:
        load.start()

    for load in loads[:1]:
        load.wait()

    @pl.loop(0, 8)
    def _(b):
        some = ups_v[pl.ds(b * 32, 32)].astype(F32)
        for t in range(4):
            wide[t, pl.ds(pl.multiple_of(b * 128, 128), 128), :] = some[:, :, t * 128 : t * 128 + 128].reshape(128, 128)

    for c in range(4):
        for t in range(4):
            uc_v[c, :, t * 128 : t * 128 + 128] = wide[t, pl.ds(c, GB, stride=4), :].astype(BF16)

    loads[1].wait()

    def term(lo, hi, c):
        return lax.dot_general(
            pooled_v[:, lo:hi], uc_v[c], (((0,), (0,)), ((), ())), preferred_element_type=F32
        )

    def keep(half, row, value):
        for part in range(2):
            acc[half, part, row : row + value.shape[0], :] = value[:, part * 256 : part * 256 + 256]

    keep(0, 0, term(384, 960, 3)[64:576])
    keep(1, 0, term(0, 128, 0))
    keep(1, 128, term(0, 256, 1)[64:192])
    keep(1, 256, term(128, 512, 2)[64:320])

    pl.semaphore_wait(barrier, len(partners))

    def span(kind, i):
        if kind == "x":
            t = lax.rem(xi + i, NX)
            return t, pl.ds(pl.multiple_of(t * 128, 128), 128)
        t = lax.rem(yi + i, NY)
        return t, pl.ds(pl.multiple_of(t * 64, 64), 64)

    def part_of(kind):
        return 0 if kind == "x" else 1

    sib_dev = at(yi, xi, other)
    steps = BOTH + (("x", 0), ("y", 0))
    sib_copies = {}
    for n, (kind, i) in enumerate(steps):
        t, rows = span(kind, i)
        part = part_of(kind)
        copy = remote(acc.at[other, part, rows], sib.at[part, rows], sib_s.at[n], sib_r.at[n], sib_dev)
        copy.start()
        sib_copies[kind, i] = copy

    def chip_sum(kind, i):
        t, rows = span(kind, i)
        part = part_of(kind)
        return acc[core, part, rows, :] + sib[part, rows, :]

    first = {}
    for kind, i in BOTH:
        sib_copies[kind, i].wait_recv()
        t, rows = span(kind, i)
        if kind == "x":
            pack(tiles_of(chip_sum(kind, i)), x1s.at[i - 1])
            copy = remote(x1s.at[i - 1], x1r.at[i - 1], x1_s.at[i - 1], x1_r.at[i - 1], at(yi, t, core))
        else:
            pack(tiles_of(chip_sum(kind, i)), y1s.at[i - 1])
            copy = remote(y1s.at[i - 1], y1r.at[i - 1], y1_s.at[i - 1], y1_r.at[i - 1], at(t, xi, core))
        copy.start()
        first[kind, i] = copy

    loads[2].wait()
    for c, ((offset, width), (block, number)) in enumerate(zip(CLASSES, BLOCKS)):
        bag = lax.dot_general(
            uc_v[c], proj_v[offset : offset + number * 128], (((1,), (1,)), ((), ())),
            preferred_element_type=F32,
        )
        for k in range(number):
            for s in range(4):
                stage[pl.ds(s * 8 + block + k, N_OWN, stride=32), :] = bag[
                    s * 64 : s * 64 + 64, k * 128 : k * 128 + 128
                ]
    abuf[...] = stage[...].reshape(N_OWN, 32, 128).astype(BF16)

    loads[3].wait()
    loads[4].wait()
    spread = lax.broadcasted_iota(jnp.int32, (GB, GB), 0)
    order = (spread & 63) * 4 + (spread >> 6)
    picked = jnp.where(order == lax.broadcasted_iota(jnp.int32, (GB, GB), 1), 1.0, 0.0).astype(BF16)
    for member in range(4):
        valid = lax.broadcasted_iota(jnp.int32, (BAG, GB), 0) < sizes_v[member : member + 1, :]
        wanted = jnp.where(valid, looks_v[member], -1)
        parts = []
        for r in range(0, GB, 64):
            ids = lax.broadcasted_iota(jnp.int32, (64, GB), 0) + r
            count = jnp.zeros((64, GB), F32)
            for l in range(BAG):
                count += jnp.where(wanted[l : l + 1, :] == ids, 1.0, 0.0)
            parts.append(count.astype(BF16))
        counts = jnp.concatenate(parts, axis=0)
        tal[member] = lax.dot_general(
            picked, counts, (((1,), (1,)), ((), ())), preferred_element_type=F32
        ).astype(BF16)

    second = {}
    sib_copies["x", 0].wait_recv()
    total = tiles_of(chip_sum("x", 0))
    for i in X_ORDER:
        first["x", i].wait_recv()
        total = [a + b for a, b in zip(total, unpack(x1r.at[i - 1], 16))]
    for k in range(8):
        pack(total[2 * k : 2 * k + 2], y2s.at[k])
    for i in Y_ORDER:
        t, rows = span("y", i)
        copy = remote(y2s.at[t], y2r.at[i - 1], y2_s.at[i - 1], y2_r.at[i - 1], at(t, xi, core))
        copy.start()
        second["y", i] = copy
    sib_copies["y", 0].wait_recv()
    total = tiles_of(chip_sum("y", 0))
    for i in Y_ORDER:
        first["y", i].wait_recv()
        total = [a + b for a, b in zip(total, unpack(y1r.at[i - 1], 8))]
    for k in range(4):
        pack(total[2 * k : 2 * k + 2], x2s.at[k])
    for i in X_ORDER:
        t, rows = span("x", i)
        copy = remote(x2s.at[t], x2r.at[i - 1], x2_s.at[i - 1], x2_r.at[i - 1], at(yi, t, core))
        copy.start()
        second["x", i] = copy

    def summed(terms):
        total = unpack(terms[0], 2)
        for term in terms[1:]:
            total = [a + b for a, b in zip(total, unpack(term, 2))]
        return total

    def near(n, mine):
        copies = []
        pack(mine, z1.at[n, zi])
        for i in (3, 2, 1):
            slot = z1.at[n, zi]
            copies.append(remote(slot, slot, z1_s.at[n, i - 1], z1_r.at[n, i - 1], z_near(i)))
            copies[-1].start()
        return copies

    def far(n):
        copies = []
        pack(summed([z1.at[n, i] for i in range(4)]), z2.at[n, zq])
        for i in (1, 2):
            slot = z2.at[n, zq]
            copies.append(remote(slot, slot, z2_s.at[n, i - 1], z2_r.at[n, i - 1], z_far(i)))
            copies[-1].start()
        return copies

    def to_owner(i):
        t = lax.rem(p + i, N_OWN)
        return remote(abuf.at[t], arecv.at[p], a_s, a_r, (g, t))

    def send_bags():
        @pl.loop(1, N_OWN)
        def _(i):
            to_owner(i).start()

        arecv[p] = abuf[p]

    z_copies = []
    waiting = []
    for n, (order, kind, own, got) in enumerate(((Y_ORDER, "y", y2s, y2r), (X_ORDER, "x", x2s, x2r))):
        for i in order:
            second[kind, i].wait_recv()
        part = summed([own.at[yi if kind == "y" else xi]] + [got.at[i - 1] for i in order])
        waiting.append(near(n, part))
        z_copies += waiting[-1]
        if n == 0:
            send_bags()

    for n in range(2):
        for copy in waiting[n]:
            copy.wait_recv()
        waiting[n] = far(n)
        z_copies += waiting[n]

    back = {}
    for n, (order, kind, gathered) in enumerate(((Y_ORDER, "y", ga), (X_ORDER, "x", gb))):
        for copy in waiting[n]:
            copy.wait_recv()
        here = yi if kind == "y" else xi
        pack([tile * scale for tile in summed([z2.at[n, i] for i in range(3)])], gathered.at[here])
        for i in order:
            t, rows = span(kind, i)
            if kind == "y":
                sems, dev = (ga_s.at[i - 1], ga_r.at[i - 1]), at(t, xi, core)
            else:
                sems, dev = (gb_s.at[i - 1], gb_r.at[i - 1]), at(yi, t, core)
            back[kind, i] = remote(gathered.at[here], gathered.at[here], *sems, dev)
            back[kind, i].start()

    last = {}
    hand = {}

    def slot(kind, half, t):
        return gx.at[half, t] if kind == "x" else gy.at[half, t]

    def to_other(kind, i, t):
        sems = (hx_s.at[i], hx_r.at[i]) if kind == "x" else (hy_s.at[i], hy_r.at[i])
        hand[kind, i] = remote(slot(kind, core, t), slot(kind, core, t), *sems, sib_dev)
        hand[kind, i].start()

    def put(kind, half, t):
        number, left, groups = (16, 0, 8) if kind == "x" else (8, 256, 4)
        tiles = unpack(slot(kind, half, t), number)

        def store(low, high, row):
            for k in range(2 * low, 2 * high):
                column = left + (k % 2) * 128
                pg_out[row + k // 2, :, column : column + 128] = tiles[k]

        plain = t * groups
        if kind == "x":
            row = half * (plain - 4 * ((t + 3) // 4)) + (1 - half) * (plain + 28)
            store(0, 4, row)

            @pl.when(t + 4 * (1 - half) > 0)
            def _():
                store(4, 8, half * (plain - 4) + (1 - half) * (plain + 28))
        else:
            row = half * (plain - 4 * ((t + 7) // 8)) + (1 - half) * (plain + 28)

            @pl.when((t - 1) * (t - 1) + (1 - half) > 0)
            def _():
                store(0, 4, row)

    def spread_out(kind, i):
        t, rows = span(kind, i)
        if kind == "x":
            sems, dev = (gx_s.at[i - 1], gx_r.at[i - 1]), at(yi, t, core)
            mine = slot("x", core, xi)
        else:
            sems, dev = (gy_s.at[i - 1], gy_r.at[i - 1]), at(t, xi, core)
            mine = slot("y", core, yi)
        last[kind, i] = remote(mine, mine, *sems, dev)
        last[kind, i].start()

    for i in X_ORDER:
        back["x", i].wait_recv()
    pack([tile for k in range(4) for tile in unpack(gb.at[k], 2)], slot("y", core, yi))
    for i in Y_ORDER:
        spread_out("y", i)
    to_other("y", 0, yi)
    for i in Y_ORDER:
        back["y", i].wait_recv()
    pack([tile for k in range(8) for tile in unpack(ga.at[k], 2)], slot("x", core, xi))
    for i in X_ORDER:
        spread_out("x", i)
    to_other("x", 0, xi)
    pltpu.make_async_copy(arecv.at[pl.ds(0, N_OWN - 1)], arecv.at[pl.ds(0, N_OWN - 1)], a_r).wait()
    loads[5].wait()
    loads[6].wait()
    stage[...] = arecv[...].astype(F32).reshape(N_OWN * 32, 128)
    for member, ((offset, width), (block, number)) in enumerate(zip(CLASSES, BLOCKS)):
        columns = []
        for k in range(number):
            columns.append(
                jnp.concatenate(
                    [stage[pl.ds(s * 8 + block + k, N_OWN, stride=32), :] for s in range(4)], axis=0
                ).astype(BF16)
            )
        bags = columns[0] if number == 1 else jnp.concatenate(columns, axis=1)
        grad = lax.dot_general(
            bags, tal[member], (((0,), (0,)), ((), ())), preferred_element_type=F32
        )[:width]
        new = state_v[member : member + 1, :] + jnp.sum(grad * grad, axis=0, keepdims=True) * (1.0 / width)
        state_out[member : member + 1, :] = new
        rows_out[offset : offset + width, :] = emb_v[offset : offset + width, :] - grad * (LEARN / jnp.sqrt(new))
    put("y", core, yi)
    put("x", core, xi)
    for kind, i in BOTH:
        last[kind, i].wait_recv()
        t = lax.rem(xi - i + NX, NX) if kind == "x" else lax.rem(yi - i + NY, NY)
        to_other(kind, i, t)
        put(kind, core, t)
    for kind, i in (("y", 0), ("x", 0)) + BOTH:
        hand[kind, i].wait_recv()
        t = lax.rem(xi - i + NX, NX) if kind == "x" else lax.rem(yi - i + NY, NY)
        put(kind, other, t)

    for group in (sib_copies, first, second, back, last, hand):
        for copy in group.values():
            copy.wait_send()
    for copy in z_copies:
        copy.wait_send()

    @pl.loop(1, N_OWN)
    def _(i):
        to_owner(i).wait_send()


def on_device(upstream, pooled, projection, embedding, row_state, lookups, bag_sizes):
    total_bags = upstream.shape[0] * lax.axis_size("grp") * lax.axis_size("own") * upstream.shape[1]
    scale = 1.0 / math.sqrt(total_bags)
    operands = (
        upstream.reshape(GB, 4, 512), pooled.reshape(GB, 960), projection, embedding.T, row_state,
        jnp.transpose(lookups[0], (0, 2, 1)), bag_sizes[0],
    )
    dma = pltpu.SemaphoreType.DMA
    any_space = pl.BlockSpec(memory_space=pl.ANY)
    scratch = [pltpu.VMEM(a.shape, a.dtype) for a in operands] + [
        pltpu.VMEM((2, 2, 512, 256), F32),
        pltpu.VMEM((2, 512, 256), F32),
        pltpu.VMEM((3, 17, 16, 128), I16),
        pltpu.VMEM((3, 17, 16, 128), I16),
        pltpu.VMEM((7, 9, 16, 128), I16),
        pltpu.VMEM((7, 9, 16, 128), I16),
        pltpu.VMEM((8, 3, 16, 128), I16),
        pltpu.VMEM((7, 3, 16, 128), I16),
        pltpu.VMEM((4, 3, 16, 128), I16),
        pltpu.VMEM((3, 3, 16, 128), I16),
        pltpu.VMEM((2, 4, 3, 16, 128), I16),
        pltpu.VMEM((2, 3, 3, 16, 128), I16),
        pltpu.VMEM((8, 3, 16, 128), I16),
        pltpu.VMEM((4, 3, 16, 128), I16),
        pltpu.VMEM((2, 4, 17, 16, 128), I16),
        pltpu.VMEM((2, 8, 9, 16, 128), I16),
        pltpu.VMEM((4, 4 * GB, 128), F32),
        pltpu.VMEM((4, GB, 512), BF16),
        pltpu.VMEM((N_OWN * 32, 128), F32),
        pltpu.VMEM((N_OWN, 32, 128), BF16),
        pltpu.VMEM((N_OWN, 32, 128), BF16),
        pltpu.VMEM((4, GB, GB), BF16),
    ] + [
        dma(n if isinstance(n, tuple) else () if n == 0 else (n,))
        for n in (7, 12, 12, 3, 3, 7, 7, 7, 7, 3, 3, (2, 3), (2, 3), (2, 2), (2, 2), 0, 0, 7, 7, 3, 3, 3, 3, 7, 7, 4, 4, 8, 8)
    ]
    rows_t, new_state, pg = pl.pallas_call(
        functools.partial(kernel, scale),
        out_shape=(
            pltpu.VMEM((960, GB), F32),
            pltpu.VMEM((4, GB), F32),
            pltpu.VMEM((60, 16, 512), F32),
        ),
        in_specs=[pl.BlockSpec(memory_space=pltpu.HBM)] * len(operands),
        out_specs=(pl.BlockSpec(memory_space=pltpu.VMEM),) * 3,
        scratch_shapes=scratch,
        compiler_params=pltpu.CompilerParams(
            collective_id=0, has_side_effects=True, vmem_limit_bytes=54 * 2**20
        ),
        name="fused",
    )(*operands)
    return rows_t.T, new_state, pg.reshape(960, 512)


def solution(mesh):
    return jax.shard_map(
        on_device,
        mesh=mesh,
        in_specs=(
            P(("grp", "own"), None, None, None),
            P(("grp", "own"), None, None),
            P(),
            P(("grp", "own"), None),
            P(None, ("grp", "own")),
            P(("grp", "own"), None, None, None),
            P(("grp", "own"), None, None),
        ),
        out_specs=(P(("grp", "own"), None), P(None, ("grp", "own")), P()),
        check_vma=False,
    )
```

```python
import functools
import math

import jax
import jax.numpy as jnp
from jax import lax
from jax.experimental import pallas as pl
from jax.experimental.pallas import tpu as pltpu
from jax.sharding import PartitionSpec as P

BAG = 16
GB = 256
LEARN = 0.05
NX, NY, NZ = 4, 8, 12
N_OWN = 64
MESH = pl.DeviceIdType.MESH
F32 = jnp.float32
BF16 = jnp.bfloat16
CLASSES = ((0, 64), (64, 128), (192, 256), (448, 512))
BLOCKS = ((0, 1), (1, 1), (2, 2), (4, 4))


I16 = jnp.int16
X_ORDER = (2, 1, 3)
Y_ORDER = (4, 3, 5, 2, 6, 1, 7)
BOTH = (("y", 4), ("y", 3), ("y", 5), ("y", 2), ("x", 2), ("y", 6), ("y", 1), ("x", 1), ("y", 7), ("x", 3))


def pack(tiles, q):
    top = jnp.abs(tiles[0])
    for tile in tiles[1:]:
        top = jnp.maximum(top, jnp.abs(tile))
    power = jnp.ceil(jnp.log2(jnp.maximum(top, 1e-30) * 1.001))
    scale = jnp.exp2(15.0 - power)
    for k, tile in enumerate(tiles):
        q[k] = jnp.round(tile * scale).astype(jnp.int32).astype(I16)
    q[len(tiles)] = power.astype(jnp.int32).astype(I16)


def unpack(q, number):
    scale = jnp.exp2(q[number].astype(jnp.int32).astype(F32) - 15.0)
    return [q[k].astype(jnp.int32).astype(F32) * scale for k in range(number)]


def tiles_of(value):
    return [
        value[r : r + 16, c : c + 128]
        for r in range(0, value.shape[0], 16)
        for c in range(0, value.shape[1], 128)
    ]


def kernel(
    scale,
    ups, pooled, proj, emb, state, looks, sizes,
    rows_out, state_out, pg_out,
    ups_v, pooled_v, proj_v, emb_v, state_v, looks_v, sizes_v,
    acc, sib, x1s, x1r, y1s, y1r, y2s, y2r, x2s, x2r, z1, z2, ga, gb, gx, gy,
    wide, uc_v, stage, abuf, arecv, tal,
    in_sem, sib_s, sib_r, x1_s, x1_r, y1_s, y1_r, y2_s, y2_r, x2_s, x2_r, z1_s, z1_r, z2_s, z2_r,
    a_s, a_r, ga_s, ga_r, gb_s, gb_r, gx_s, gx_r, gy_s, gy_r, hx_s, hx_r, hy_s, hy_r,
):
    g = lax.axis_index("grp")
    p = lax.axis_index("own")
    core = lax.rem(p, 2)
    xi = lax.rem(p // 2, NX)
    yi = p // (2 * NX)
    zq = g // 4
    zi = lax.rem(g, 4)
    other = 1 - core

    def at(y, x, c):
        return (g, (y * NX + x) * 2 + c)

    def remote(src, dst, send, recv, dev):
        return pltpu.make_async_remote_copy(
            src_ref=src, dst_ref=dst, send_sem=send, recv_sem=recv,
            device_id=dev, device_id_type=MESH,
        )

    ins = (
        (ups, ups_v), (pooled, pooled_v), (proj, proj_v), (looks, looks_v), (sizes, sizes_v), (emb, emb_v), (state, state_v),
    )
    barrier = pltpu.get_barrier_semaphore()

    def z_near(i):
        return (zq * 4 + lax.rem(zi + i, 4), p)

    def z_far(i):
        return (lax.rem(g + 4 * i, NZ), p)

    partners = (
        [at(lax.rem(yi + i, NY), xi, core) for i in Y_ORDER]
        + [at(yi, lax.rem(xi + i, NX), core) for i in X_ORDER]
        + [at(yi, xi, other)]
        + [z_far(i) for i in (1, 2)]
        + [z_near(i) for i in (2, 1, 3)]
    )
    for dev in partners:
        pl.semaphore_signal(barrier, inc=1, device_id=dev, device_id_type=MESH)

    loads = [pltpu.make_async_copy(a, b, in_sem.at[i]) for i, (a, b) in enumerate(ins)]
    for load in loads:
        load.start()

    for load in loads[:1]:
        load.wait()

    @pl.loop(0, 8)
    def _(b):
        some = ups_v[pl.ds(b * 32, 32)].astype(F32)
        for t in range(4):
            wide[t, pl.ds(pl.multiple_of(b * 128, 128), 128), :] = some[:, :, t * 128 : t * 128 + 128].reshape(128, 128)

    for c in range(4):
        for t in range(4):
            uc_v[c, :, t * 128 : t * 128 + 128] = wide[t, pl.ds(c, GB, stride=4), :].astype(BF16)

    loads[1].wait()

    def term(lo, hi, c):
        return lax.dot_general(
            pooled_v[:, lo:hi], uc_v[c], (((0,), (0,)), ((), ())), preferred_element_type=F32
        )

    def keep(half, row, value):
        for part in range(2):
            acc[half, part, row : row + value.shape[0], :] = value[:, part * 256 : part * 256 + 256]

    keep(0, 0, term(384, 960, 3)[64:576])
    keep(1, 0, term(0, 128, 0))
    keep(1, 128, term(0, 256, 1)[64:192])
    keep(1, 256, term(128, 512, 2)[64:320])

    pl.semaphore_wait(barrier, len(partners))

    def span(kind, i):
        if kind == "x":
            t = lax.rem(xi + i, NX)
            return t, pl.ds(pl.multiple_of(t * 128, 128), 128)
        t = lax.rem(yi + i, NY)
        return t, pl.ds(pl.multiple_of(t * 64, 64), 64)

    def part_of(kind):
        return 0 if kind == "x" else 1

    sib_dev = at(yi, xi, other)
    steps = BOTH + (("x", 0), ("y", 0))
    sib_copies = {}
    for n, (kind, i) in enumerate(steps):
        t, rows = span(kind, i)
        part = part_of(kind)
        copy = remote(acc.at[other, part, rows], sib.at[part, rows], sib_s.at[n], sib_r.at[n], sib_dev)
        copy.start()
        sib_copies[kind, i] = copy

    def chip_sum(kind, i):
        t, rows = span(kind, i)
        part = part_of(kind)
        return acc[core, part, rows, :] + sib[part, rows, :]

    first = {}
    for kind, i in BOTH:
        sib_copies[kind, i].wait_recv()
        t, rows = span(kind, i)
        if kind == "x":
            pack(tiles_of(chip_sum(kind, i)), x1s.at[i - 1])
            copy = remote(x1s.at[i - 1], x1r.at[i - 1], x1_s.at[i - 1], x1_r.at[i - 1], at(yi, t, core))
        else:
            pack(tiles_of(chip_sum(kind, i)), y1s.at[i - 1])
            copy = remote(y1s.at[i - 1], y1r.at[i - 1], y1_s.at[i - 1], y1_r.at[i - 1], at(t, xi, core))
        copy.start()
        first[kind, i] = copy

    loads[2].wait()
    for c, ((offset, width), (block, number)) in enumerate(zip(CLASSES, BLOCKS)):
        bag = lax.dot_general(
            uc_v[c], proj_v[offset : offset + number * 128], (((1,), (1,)), ((), ())),
            preferred_element_type=F32,
        )
        for k in range(number):
            for s in range(4):
                stage[pl.ds(s * 8 + block + k, N_OWN, stride=32), :] = bag[
                    s * 64 : s * 64 + 64, k * 128 : k * 128 + 128
                ]
    abuf[...] = stage[...].reshape(N_OWN, 32, 128).astype(BF16)

    loads[3].wait()
    loads[4].wait()
    spread = lax.broadcasted_iota(jnp.int32, (GB, GB), 0)
    order = (spread & 63) * 4 + (spread >> 6)
    picked = jnp.where(order == lax.broadcasted_iota(jnp.int32, (GB, GB), 1), 1.0, 0.0).astype(BF16)
    for member in range(4):
        valid = lax.broadcasted_iota(jnp.int32, (BAG, GB), 0) < sizes_v[member : member + 1, :]
        wanted = jnp.where(valid, looks_v[member], -1)
        parts = []
        for r in range(0, GB, 64):
            ids = lax.broadcasted_iota(jnp.int32, (64, GB), 0) + r
            count = jnp.zeros((64, GB), F32)
            for l in range(BAG):
                count += jnp.where(wanted[l : l + 1, :] == ids, 1.0, 0.0)
            parts.append(count.astype(BF16))
        counts = jnp.concatenate(parts, axis=0)
        tal[member] = lax.dot_general(
            picked, counts, (((1,), (1,)), ((), ())), preferred_element_type=F32
        ).astype(BF16)

    second = {}
    sib_copies["x", 0].wait_recv()
    total = tiles_of(chip_sum("x", 0))
    for i in X_ORDER:
        first["x", i].wait_recv()
        total = [a + b for a, b in zip(total, unpack(x1r.at[i - 1], 16))]
    for k in range(8):
        pack(total[2 * k : 2 * k + 2], y2s.at[k])
    for i in Y_ORDER:
        t, rows = span("y", i)
        copy = remote(y2s.at[t], y2r.at[i - 1], y2_s.at[i - 1], y2_r.at[i - 1], at(t, xi, core))
        copy.start()
        second["y", i] = copy
    sib_copies["y", 0].wait_recv()
    total = tiles_of(chip_sum("y", 0))
    for i in Y_ORDER:
        first["y", i].wait_recv()
        total = [a + b for a, b in zip(total, unpack(y1r.at[i - 1], 8))]
    for k in range(4):
        pack(total[2 * k : 2 * k + 2], x2s.at[k])
    for i in X_ORDER:
        t, rows = span("x", i)
        copy = remote(x2s.at[t], x2r.at[i - 1], x2_s.at[i - 1], x2_r.at[i - 1], at(yi, t, core))
        copy.start()
        second["x", i] = copy

    def to_owner(dy, dx, dc):
        t = (lax.rem(yi + dy, NY) * NX + lax.rem(xi + dx, NX)) * 2 + lax.rem(core + dc, 2)
        return remote(abuf.at[t], arecv.at[p], a_s, a_r, (g, t))

    def send_bags(act, which):
        if which == 0:

            @pl.loop(0, 14)
            def _(m):
                act(to_owner(1 + m // 2, 0, lax.rem(m, 2)))

            @pl.loop(1, 8)
            def _(m):
                act(to_owner(0, m // 2, lax.rem(m, 2)))
        else:

            @pl.loop(0, 42)
            def _(m):
                act(to_owner(1 + m // 6, 1 + lax.rem(m, 6) // 2, lax.rem(m, 2)))

    send_bags(lambda copy: copy.start(), 0)
    arecv[p] = abuf[p]

    def summed(terms):
        total = unpack(terms[0], 2)
        for term in terms[1:]:
            total = [a + b for a, b in zip(total, unpack(term, 2))]
        return total

    def near(n, mine):
        copies = []
        pack(mine, z1.at[n, zi])
        for i in (3, 2, 1):
            slot = z1.at[n, zi]
            copies.append(remote(slot, slot, z1_s.at[n, i - 1], z1_r.at[n, i - 1], z_near(i)))
            copies[-1].start()
        return copies

    def far(n):
        copies = []
        pack(summed([z1.at[n, i] for i in range(4)]), z2.at[n, zq])
        for i in (1, 2):
            slot = z2.at[n, zq]
            copies.append(remote(slot, slot, z2_s.at[n, i - 1], z2_r.at[n, i - 1], z_far(i)))
            copies[-1].start()
        return copies

    z_copies = []
    waiting = []
    for n, (order, kind, own, got) in enumerate(((Y_ORDER, "y", y2s, y2r), (X_ORDER, "x", x2s, x2r))):
        for i in order:
            second[kind, i].wait_recv()
        part = summed([own.at[yi if kind == "y" else xi]] + [got.at[i - 1] for i in order])
        waiting.append(near(n, part))
        z_copies += waiting[-1]
        if n == 0:
            send_bags(lambda copy: copy.start(), 1)

    for n in range(2):
        for copy in waiting[n]:
            copy.wait_recv()
        waiting[n] = far(n)
        z_copies += waiting[n]

    back = {}
    for n, (order, kind, gathered) in enumerate(((Y_ORDER, "y", ga), (X_ORDER, "x", gb))):
        for copy in waiting[n]:
            copy.wait_recv()
        here = yi if kind == "y" else xi
        pack([tile * scale for tile in summed([z2.at[n, i] for i in range(3)])], gathered.at[here])
        for i in order:
            t, rows = span(kind, i)
            if kind == "y":
                sems, dev = (ga_s.at[i - 1], ga_r.at[i - 1]), at(t, xi, core)
            else:
                sems, dev = (gb_s.at[i - 1], gb_r.at[i - 1]), at(yi, t, core)
            back[kind, i] = remote(gathered.at[here], gathered.at[here], *sems, dev)
            back[kind, i].start()

    last = {}
    hand = {}

    def slot(kind, half, t):
        return gx.at[half, t] if kind == "x" else gy.at[half, t]

    def to_other(kind, i, t):
        sems = (hx_s.at[i], hx_r.at[i]) if kind == "x" else (hy_s.at[i], hy_r.at[i])
        hand[kind, i] = remote(slot(kind, core, t), slot(kind, core, t), *sems, sib_dev)
        hand[kind, i].start()

    def put(kind, half, t):
        number, left, groups = (16, 0, 8) if kind == "x" else (8, 256, 4)
        tiles = unpack(slot(kind, half, t), number)

        def store(low, high, row):
            for k in range(2 * low, 2 * high):
                column = left + (k % 2) * 128
                pg_out[row + k // 2, :, column : column + 128] = tiles[k]

        plain = t * groups
        if kind == "x":
            row = half * (plain - 4 * ((t + 3) // 4)) + (1 - half) * (plain + 28)
            store(0, 4, row)

            @pl.when(t + 4 * (1 - half) > 0)
            def _():
                store(4, 8, half * (plain - 4) + (1 - half) * (plain + 28))
        else:
            row = half * (plain - 4 * ((t + 7) // 8)) + (1 - half) * (plain + 28)

            @pl.when((t - 1) * (t - 1) + (1 - half) > 0)
            def _():
                store(0, 4, row)

    def spread_out(kind, i):
        t, rows = span(kind, i)
        if kind == "x":
            sems, dev = (gx_s.at[i - 1], gx_r.at[i - 1]), at(yi, t, core)
            mine = slot("x", core, xi)
        else:
            sems, dev = (gy_s.at[i - 1], gy_r.at[i - 1]), at(t, xi, core)
            mine = slot("y", core, yi)
        last[kind, i] = remote(mine, mine, *sems, dev)
        last[kind, i].start()

    for i in X_ORDER:
        back["x", i].wait_recv()
    pack([tile for k in range(4) for tile in unpack(gb.at[k], 2)], slot("y", core, yi))
    for i in Y_ORDER:
        spread_out("y", i)
    to_other("y", 0, yi)
    for i in Y_ORDER:
        back["y", i].wait_recv()
    pack([tile for k in range(8) for tile in unpack(ga.at[k], 2)], slot("x", core, xi))
    for i in X_ORDER:
        spread_out("x", i)
    to_other("x", 0, xi)
    put("y", core, yi)
    put("x", core, xi)
    for kind, i in (("x", 1), ("x", 3), ("x", 2), ("y", 1), ("y", 7), ("y", 2), ("y", 6), ("y", 3), ("y", 5), ("y", 4)):
        last[kind, i].wait_recv()
        t = lax.rem(xi - i + NX, NX) if kind == "x" else lax.rem(yi - i + NY, NY)
        to_other(kind, i, t)
        put(kind, core, t)
    pltpu.make_async_copy(arecv.at[pl.ds(0, N_OWN - 1)], arecv.at[pl.ds(0, N_OWN - 1)], a_r).wait()
    loads[5].wait()
    loads[6].wait()
    stage[...] = arecv[...].astype(F32).reshape(N_OWN * 32, 128)
    for member, ((offset, width), (block, number)) in enumerate(zip(CLASSES, BLOCKS)):
        columns = []
        for k in range(number):
            columns.append(
                jnp.concatenate(
                    [stage[pl.ds(s * 8 + block + k, N_OWN, stride=32), :] for s in range(4)], axis=0
                ).astype(BF16)
            )
        bags = columns[0] if number == 1 else jnp.concatenate(columns, axis=1)
        grad = lax.dot_general(
            bags, tal[member], (((0,), (0,)), ((), ())), preferred_element_type=F32
        )[:width]
        new = state_v[member : member + 1, :] + jnp.sum(grad * grad, axis=0, keepdims=True) * (1.0 / width)
        state_out[member : member + 1, :] = new
        rows_out[offset : offset + width, :] = emb_v[offset : offset + width, :] - grad * (LEARN / jnp.sqrt(new))
    for kind, i in (("y", 0), ("x", 0)) + BOTH:
        hand[kind, i].wait_recv()
        t = lax.rem(xi - i + NX, NX) if kind == "x" else lax.rem(yi - i + NY, NY)
        put(kind, other, t)

    for group in (sib_copies, first, second, back, last, hand):
        for copy in group.values():
            copy.wait_send()
    for copy in z_copies:
        copy.wait_send()

    send_bags(lambda copy: copy.wait_send(), 0)
    send_bags(lambda copy: copy.wait_send(), 1)


def on_device(upstream, pooled, projection, embedding, row_state, lookups, bag_sizes):
    total_bags = upstream.shape[0] * lax.axis_size("grp") * lax.axis_size("own") * upstream.shape[1]
    scale = 1.0 / math.sqrt(total_bags)
    operands = (
        upstream.reshape(GB, 4, 512), pooled.reshape(GB, 960), projection, embedding.T, row_state,
        jnp.transpose(lookups[0], (0, 2, 1)), bag_sizes[0],
    )
    dma = pltpu.SemaphoreType.DMA
    any_space = pl.BlockSpec(memory_space=pl.ANY)
    scratch = [pltpu.VMEM(a.shape, a.dtype) for a in operands] + [
        pltpu.VMEM((2, 2, 512, 256), F32),
        pltpu.VMEM((2, 512, 256), F32),
        pltpu.VMEM((3, 17, 16, 128), I16),
        pltpu.VMEM((3, 17, 16, 128), I16),
        pltpu.VMEM((7, 9, 16, 128), I16),
        pltpu.VMEM((7, 9, 16, 128), I16),
        pltpu.VMEM((8, 3, 16, 128), I16),
        pltpu.VMEM((7, 3, 16, 128), I16),
        pltpu.VMEM((4, 3, 16, 128), I16),
        pltpu.VMEM((3, 3, 16, 128), I16),
        pltpu.VMEM((2, 4, 3, 16, 128), I16),
        pltpu.VMEM((2, 3, 3, 16, 128), I16),
        pltpu.VMEM((8, 3, 16, 128), I16),
        pltpu.VMEM((4, 3, 16, 128), I16),
        pltpu.VMEM((2, 4, 17, 16, 128), I16),
        pltpu.VMEM((2, 8, 9, 16, 128), I16),
        pltpu.VMEM((4, 4 * GB, 128), F32),
        pltpu.VMEM((4, GB, 512), BF16),
        pltpu.VMEM((N_OWN * 32, 128), F32),
        pltpu.VMEM((N_OWN, 32, 128), BF16),
        pltpu.VMEM((N_OWN, 32, 128), BF16),
        pltpu.VMEM((4, GB, GB), BF16),
    ] + [
        dma(n if isinstance(n, tuple) else () if n == 0 else (n,))
        for n in (7, 12, 12, 3, 3, 7, 7, 7, 7, 3, 3, (2, 3), (2, 3), (2, 2), (2, 2), 0, 0, 7, 7, 3, 3, 3, 3, 7, 7, 4, 4, 8, 8)
    ]
    rows_t, new_state, pg = pl.pallas_call(
        functools.partial(kernel, scale),
        out_shape=(
            pltpu.VMEM((960, GB), F32),
            pltpu.VMEM((4, GB), F32),
            pltpu.VMEM((60, 16, 512), F32),
        ),
        in_specs=[pl.BlockSpec(memory_space=pltpu.HBM)] * len(operands),
        out_specs=(pl.BlockSpec(memory_space=pltpu.VMEM),) * 3,
        scratch_shapes=scratch,
        compiler_params=pltpu.CompilerParams(
            collective_id=0, has_side_effects=True, vmem_limit_bytes=54 * 2**20
        ),
        name="fused",
    )(*operands)
    return rows_t.T, new_state, pg.reshape(960, 512)


def solution(mesh):
    return jax.shard_map(
        on_device,
        mesh=mesh,
        in_specs=(
            P(("grp", "own"), None, None, None),
            P(("grp", "own"), None, None),
            P(),
            P(("grp", "own"), None),
            P(None, ("grp", "own")),
            P(("grp", "own"), None, None, None),
            P(("grp", "own"), None, None),
        ),
        out_specs=(P(("grp", "own"), None), P(None, ("grp", "own")), P()),
        check_vma=False,
    )
```
